512 devices in a mesh: hist: 32 (over x, y), col: 16 (over z, core).
Axes of the slice: x: 4, y: 8, z: 8, core: 2. Of those that a mesh axis runs over, the one named last changes fastest.
Arguments:
- less_row: bfloat16 [2, 128, 128, 4096], P(None, None, 'col', 'hist'), may hold values from -1.796875 to 1.796875
- less_col: bfloat16 [2, 128, 128, 4096], P(None, None, 'col', 'hist'), may hold values from -1.796875 to 1.796875
- great_row: bfloat16 [2, 128, 128, 4096], P(None, None, 'col', 'hist'), may hold values from -1.796875 to 1.796875
- great_col: bfloat16 [2, 128, 128, 4096], P(None, None, 'col', 'hist'), may hold values from -1.796875 to 1.796875
- density: float32 [2, 128, 128], replicated, may hold values from -1.8 to 1.8
- hamiltonian: float32 [128, 128], replicated, may hold values from -0.5 to 0.5
Outputs:
- less_row_out: bfloat16 [2, 128, 128, 4096], P(None, None, 'col', 'hist')
- less_col_out: bfloat16 [2, 128, 128, 4096], P(None, None, 'col', 'hist')
- great_row_out: bfloat16 [2, 128, 128, 4096], P(None, None, 'col', 'hist')
- great_col_out: bfloat16 [2, 128, 128, 4096], P(None, None, 'col', 'hist')
- density_out: float32 [2, 128, 128], replicated
The draws below stay inside these ranges and needn't reach their ends.
All inputs are finite; a program needn't handle non-finite values.
Results may differ from the reference program's by a relative error of at most 0.033.
Values may be sent and summed in bfloat16 or wider, within the bound.
A program may use at most 64 MiB of HBM per device.

```python
import jax
import jax.numpy as jnp
from jax import lax

NORB = 128
STEPS = 3
HIST = 4096


def block_levels(own_key, shape, shards, smallest, top_value):
    gain, own = 1.0, jax.random.fold_in(own_key, 6)
    for position, shards_of in shards:
        heights = jnp.exp(jax.random.uniform(jax.random.fold_in(own, position), (shards_of,), jnp.float32, smallest / len(shards), top_value / len(shards)))
        gain = gain * jnp.repeat(heights, shape[position] // shards_of).reshape([-1 if axis == position else 1 for axis in range(len(shape))])
    return gain


def normal_values(rng, extent, width, bound, cuts=(), kind=jnp.bfloat16):
    entries = width * jax.random.normal(rng, extent, jnp.float32)
    if cuts:
        entries = entries * block_levels(rng, extent, cuts, -0.22, 0.18)
    return jnp.clip(entries, -bound, bound).astype(kind)


def setup_inputs(seed: int = 0) -> dict:
    seeds = jax.random.split(jax.random.key(seed), 7)
    less_row = normal_values(seeds[0], (2, NORB, NORB, HIST), 0.3, 1.796875, ((2, 16), (3, 32)))
    less_col = normal_values(seeds[1], (2, NORB, NORB, HIST), 0.3, 1.796875, ((2, 16), (3, 32)))
    great_row = normal_values(seeds[2], (2, NORB, NORB, HIST), 0.3, 1.796875, ((2, 16), (3, 32)))
    great_col = normal_values(seeds[3], (2, NORB, NORB, HIST), 0.3, 1.796875, ((2, 16), (3, 32)))
    density = normal_values(seeds[4], (2, NORB, NORB), 0.3, 1.8, (), jnp.float32)
    hamiltonian = normal_values(seeds[5], (NORB, NORB), NORB ** -0.5, 0.5, (), jnp.float32)
    return dict(less_row=less_row, less_col=less_col, great_row=great_row, great_col=great_col, density=density, hamiltonian=hamiltonian)


step_length = 0.1
mean_field = 2.0
coupling = 1.0

def unitary(hamiltonian, density):
    sym_ham = 0.5 * (hamiltonian + hamiltonian.T) + mean_field * jnp.diag(jnp.diagonal(density[0]))
    halved = 0.5 * step_length * sym_ham
    squared = jnp.dot(halved, halved, precision=lax.Precision.HIGHEST)
    identity = jnp.eye(sym_ham.shape[0], dtype=jnp.float32)
    factor = jnp.linalg.cholesky(identity + squared)
    unit_real = jax.scipy.linalg.cho_solve((factor, True), identity - squared)
    unit_imag = jax.scipy.linalg.cho_solve((factor, True), -2.0 * halved)
    return (unit_real, unit_imag)

def self_energy(row_hist, col_turned):
    green_real = row_hist[0].astype(jnp.float32)
    green_imag = row_hist[1].astype(jnp.float32)
    other_real = col_turned[0].astype(jnp.float32)
    other_imag = col_turned[1].astype(jnp.float32)
    square_real = green_real * green_real - green_imag * green_imag
    square_imag = 2.0 * green_real * green_imag
    out_real = coupling * coupling * (square_real * other_real - square_imag * other_imag)
    out_imag = coupling * coupling * (square_real * other_imag + square_imag * other_real)
    return jnp.stack([out_real, out_imag]).astype(jnp.bfloat16)

def contract_pair(first, second):
    return jnp.einsum('ikt,kjt->ij', first.astype(jnp.float32), second.astype(jnp.float32))

def contract(sigma, column):
    real_part = contract_pair(sigma[0], column[0]) - contract_pair(sigma[1], column[1])
    imag_part = contract_pair(sigma[0], column[1]) + contract_pair(sigma[1], column[0])
    return jnp.stack([real_part, imag_part])

def rotate_density(unit_real, unit_imag, rho):
    high = lax.Precision.HIGHEST
    left_real = jnp.dot(unit_real, rho[0], precision=high) - jnp.dot(unit_imag, rho[1], precision=high)
    left_imag = jnp.dot(unit_real, rho[1], precision=high) + jnp.dot(unit_imag, rho[0], precision=high)
    out_real = jnp.dot(left_real, unit_real.T, precision=high) + jnp.dot(left_imag, unit_imag.T, precision=high)
    out_imag = jnp.dot(left_imag, unit_real.T, precision=high) - jnp.dot(left_real, unit_imag.T, precision=high)
    return jnp.stack([out_real, out_imag])

def advance_rows(low_real, low_imag, history):
    count = history.shape[1]
    hist_real = history[0].reshape(count, -1)
    hist_imag = history[1].reshape(count, -1)
    out_real = jnp.dot(low_real.astype(jnp.float32), hist_real.astype(jnp.float32), preferred_element_type=jnp.float32) - jnp.dot(low_imag.astype(jnp.float32), hist_imag.astype(jnp.float32), preferred_element_type=jnp.float32)
    out_imag = jnp.dot(low_real.astype(jnp.float32), hist_imag.astype(jnp.float32), preferred_element_type=jnp.float32) + jnp.dot(low_imag.astype(jnp.float32), hist_real.astype(jnp.float32), preferred_element_type=jnp.float32)
    return jnp.stack([out_real, out_imag]).astype(jnp.bfloat16).reshape(history.shape)

def right_pair(first, matrix):
    return jnp.einsum('imt,jm->ijt', first.astype(jnp.float32), matrix.astype(jnp.float32))

def advance_cols(low_real, low_imag, history):
    out_real = right_pair(history[0], low_real) + right_pair(history[1], low_imag)
    out_imag = right_pair(history[1], low_real) - right_pair(history[0], low_imag)
    return jnp.stack([out_real, out_imag]).astype(jnp.bfloat16)

def reference(less_row, less_col, great_row, great_col, density, hamiltonian):
    rho = density
    for step_index in range(STEPS):
        unit_real, unit_imag = unitary(hamiltonian, rho)
        sigma_less = self_energy(less_row, jnp.swapaxes(great_col, 1, 2))
        sigma_great = self_energy(great_row, jnp.swapaxes(less_col, 1, 2))
        collision = step_length * (contract(sigma_great, less_col) - contract(sigma_less, great_col))
        rho = rotate_density(unit_real, unit_imag, rho) + collision
        low_real = unit_real.astype(jnp.bfloat16)
        low_imag = unit_imag.astype(jnp.bfloat16)
        less_row = advance_rows(low_real, low_imag, less_row)
        great_row = advance_rows(low_real, low_imag, great_row)
        less_col = advance_cols(low_real, low_imag, less_col)
        great_col = advance_cols(low_real, low_imag, great_col)
    return (less_row, less_col, great_row, great_col, rho)
```

```python
import jax
import jax.numpy as jnp
from jax import lax
from jax.experimental import pallas as pl
from jax.experimental.pallas import tpu as pltpu
from jax.sharding import PartitionSpec as P

STEPS = 3


step_length = 0.1
mean_field = 2.0
coupling = 1.0


def in_one_piece(arrays, axis, split_dim, concat_dim, along):
    ends, at = ([], 0)
    for a in arrays[:-1]:
        at += a.shape[along]
        ends.append(at)
    both = jnp.concatenate(arrays, axis=along)
    return tuple(
        jnp.split(
            lax.all_to_all(both, axis, split_axis=split_dim, concat_axis=concat_dim, tiled=True),
            ends,
            axis=along,
        )
    )


def split_up(array, dim, size):
    lengths = array.shape
    parts = array.reshape(*lengths[:dim], size, lengths[dim] // size, *lengths[dim + 1 :])
    return jnp.moveaxis(parts, dim, 0)


def summed_on_arrival(array, axis, dim):
    size = lax.axis_size(axis)
    parts = lax.all_to_all(split_up(array, dim, size), axis, 0, 0, tiled=True)
    return jnp.sum(parts.astype(jnp.float32), axis=0)


def from_everyone(array, axis):
    size = lax.axis_size(axis)
    return lax.all_to_all(
        jnp.broadcast_to(array[None], (size, *array.shape)), axis, 0, 0, tiled=True
    )


def over_copies(array, axis):
    return from_everyone(array, axis).sum(axis=0)


def joined_along(parts, dim):
    parts = jnp.moveaxis(parts, 0, dim)
    lengths = parts.shape
    return parts.reshape(*lengths[:dim], lengths[dim] * lengths[dim + 1], *lengths[dim + 2 :])


def gather_directly(array, axis, dim):
    return joined_along(from_everyone(array, axis), dim)


def unitary(hamiltonian, density):
    sym_ham = 0.5 * (hamiltonian + hamiltonian.T) + mean_field * jnp.diag(jnp.diagonal(density[0]))
    halved = 0.5 * step_length * sym_ham
    squared = jnp.dot(halved, halved, precision=lax.Precision.HIGHEST)
    identity = jnp.eye(sym_ham.shape[0], dtype=jnp.float32)
    factor = jnp.linalg.cholesky(identity + squared)
    unit_real = jax.scipy.linalg.cho_solve((factor, True), identity - squared)
    unit_imag = jax.scipy.linalg.cho_solve((factor, True), -2.0 * halved)
    return (unit_real, unit_imag)


def self_energy(row_hist, col_turned):
    green_real = row_hist[0].astype(jnp.float32)
    green_imag = row_hist[1].astype(jnp.float32)
    other_real = col_turned[0].astype(jnp.float32)
    other_imag = col_turned[1].astype(jnp.float32)
    square_real = green_real * green_real - green_imag * green_imag
    square_imag = 2.0 * green_real * green_imag
    out_real = coupling * coupling * (square_real * other_real - square_imag * other_imag)
    out_imag = coupling * coupling * (square_real * other_imag + square_imag * other_real)
    return jnp.stack([out_real, out_imag]).astype(jnp.bfloat16)


def contract_pair(first, second):
    return jnp.einsum("ikt,kjt->ij", first, second, preferred_element_type=jnp.float32)


def contract(sigma, rows_block):
    real_part = contract_pair(sigma[0], rows_block[0]) - contract_pair(sigma[1], rows_block[1])
    imag_part = contract_pair(sigma[0], rows_block[1]) + contract_pair(sigma[1], rows_block[0])
    return jnp.stack([real_part, imag_part])


def rotate_density(unit_real, unit_imag, rho):
    high = lax.Precision.HIGHEST
    left_real = jnp.dot(unit_real, rho[0], precision=high) - jnp.dot(
        unit_imag, rho[1], precision=high
    )
    left_imag = jnp.dot(unit_real, rho[1], precision=high) + jnp.dot(
        unit_imag, rho[0], precision=high
    )
    out_real = jnp.dot(left_real, unit_real.T, precision=high) + jnp.dot(
        left_imag, unit_imag.T, precision=high
    )
    out_imag = jnp.dot(left_imag, unit_real.T, precision=high) - jnp.dot(
        left_real, unit_imag.T, precision=high
    )
    return jnp.stack([out_real, out_imag])


def advance_rows(low_real, low_imag, history):
    count = history.shape[1]
    hist_real = history[0].reshape(count, -1)
    hist_imag = history[1].reshape(count, -1)
    out_real = jnp.dot(low_real, hist_real, preferred_element_type=jnp.float32) - jnp.dot(
        low_imag, hist_imag, preferred_element_type=jnp.float32
    )
    out_imag = jnp.dot(low_real, hist_imag, preferred_element_type=jnp.float32) + jnp.dot(
        low_imag, hist_real, preferred_element_type=jnp.float32
    )
    return jnp.stack([out_real, out_imag]).astype(jnp.bfloat16).reshape(history.shape)


def right_pair(first, matrix):
    return jnp.einsum("imt,jm->ijt", first, matrix, preferred_element_type=jnp.float32)


def advance_cols(low_real, low_imag, rows_block):
    out_real = right_pair(rows_block[0], low_real) + right_pair(rows_block[1], low_imag)
    out_imag = right_pair(rows_block[1], low_real) - right_pair(rows_block[0], low_imag)
    return jnp.stack([out_real, out_imag]).astype(jnp.bfloat16)


def direct_steps(less_row, less_col, great_row, great_col, density, hamiltonian):
    rho = density
    rows_less, rows_great = in_one_piece((less_col, great_col), "col", 1, 2, 0)
    for step_index in range(STEPS):
        unit_real, unit_imag = unitary(hamiltonian, rho)
        sigma_less = self_energy(less_row, jnp.swapaxes(rows_great, 1, 2))
        sigma_great = self_energy(great_row, jnp.swapaxes(rows_less, 1, 2))
        partial_sum = step_length * (
            contract(sigma_great, rows_less) - contract(sigma_less, rows_great)
        )
        rotated = rotate_density(unit_real, unit_imag, rho)
        column_piece = summed_on_arrival(partial_sum.astype(jnp.bfloat16), "col", 2)
        column_piece = over_copies(column_piece, "hist")
        width = column_piece.shape[2]
        start = lax.axis_index("col") * width
        own_block = lax.dynamic_slice_in_dim(rotated, start, width, 2) + column_piece
        rho = gather_directly(own_block, "col", 2)
        low_real = unit_real.astype(jnp.bfloat16)
        low_imag = unit_imag.astype(jnp.bfloat16)
        less_row = advance_rows(low_real, low_imag, less_row)
        great_row = advance_rows(low_real, low_imag, great_row)
        rows_less = advance_cols(low_real, low_imag, rows_less)
        rows_great = advance_cols(low_real, low_imag, rows_great)
    less_col, great_col = (
        lax.all_to_all(rows_less, "col", split_axis=2, concat_axis=1, tiled=True),
        lax.all_to_all(rows_great, "col", split_axis=2, concat_axis=1, tiled=True),
    )
    return (less_row, less_col, great_row, great_col, rho)


NORB = 128
BF = jnp.bfloat16
F32 = jnp.float32
MESH = pl.DeviceIdType.MESH
COL_PEERS = [(dz, dc) for dz in (4, 3, 5, 2, 6, 1, 7) for dc in (0, 1)] + [(0, 1)]
RESIDUAL_MAX = 3e-4


def split_terms(x):
    high = x.astype(BF)
    return high, (x - high.astype(F32)).astype(BF)


def fine_dot(a, b):
    ah, al = split_terms(a)
    bh, bl = split_terms(b)

    def one(p, q):
        return jnp.dot(p, q, preferred_element_type=F32)

    return one(ah, bh) + (one(ah, bl) + one(al, bh))


def parts_of(product, at):
    rr = product[at : at + NORB, :NORB]
    ri = product[at : at + NORB, NORB:]
    ir = product[at + NORB : at + 2 * NORB, :NORB]
    ii = product[at + NORB : at + 2 * NORB, NORB:]
    return rr, ri, ir, ii


def complex_dots(lefts, right):
    rows = jnp.concatenate([x for left in lefts for x in left], axis=0)
    product = fine_dot(rows, jnp.concatenate(right, axis=1))
    outs = []
    for n in range(len(lefts)):
        rr, ri, ir, ii = parts_of(product, 2 * NORB * n)
        outs.append((rr - ii, ri + ir))
    return outs


def rotate(unit, rho):
    left = complex_dots([unit], rho)[0]
    product = fine_dot(jnp.concatenate(left, axis=0), jnp.concatenate(unit, axis=1))
    rr, ri, ir, ii = parts_of(product, 0)
    return rr + ii, ir - ri


def crank_nicolson(eye, off, diag_row, diag_col):
    inv_re_col = 1.0 / (1.0 + diag_col * diag_col)
    inv_im_col = -diag_col * inv_re_col
    inv_re_row = 1.0 / (1.0 + diag_row * diag_row)
    inv_im_row = -diag_row * inv_re_row
    power = (inv_im_col * off, -inv_re_col * off)
    total = (eye + power[0], power[1])
    power = complex_dots([power], power)[0]
    for last in (False, False, True):
        if last:
            gain = complex_dots([total], power)[0]
        else:
            following, gain = complex_dots([power, total], power)
            power = following
        total = (total[0] + gain[0], total[1] + gain[1])
    inverse = (
        total[0] * inv_re_row - total[1] * inv_im_row,
        total[0] * inv_im_row + total[1] * inv_re_row,
    )
    return (2.0 * inverse[0] - eye, 2.0 * inverse[1])


def residual_of(eye, off, diag_col, unit):
    inverse = (0.5 * (unit[0] + eye), 0.5 * unit[1])
    rows = off + eye * diag_col
    product = fine_dot(rows, jnp.concatenate(inverse, axis=1))
    rest_re = inverse[0] - product[:, NORB:] - eye
    rest_im = inverse[1] + product[:, :NORB]
    sums = jnp.sum(jnp.abs(rest_re) + jnp.abs(rest_im), axis=1, keepdims=True)
    return jnp.max(sums, axis=0, keepdims=True)


def stacked_low(unit, sign):
    low_re, low_im = unit[0].astype(BF), (sign * unit[1]).astype(BF)
    top = jnp.concatenate([low_re, -low_im], axis=1)
    bottom = jnp.concatenate([low_im, low_re], axis=1)
    return jnp.concatenate([top, bottom], axis=0)


def pair_of(ref, a, k):
    sides = []
    for kk in (k, k + 1):
        planes = [ref[a, comp, kk].reshape(NORB, NORB) for comp in (0, 1)]
        sides.append(jnp.concatenate(planes, axis=0))
    return jnp.concatenate(sides, axis=1)


def advance(weights, src, dst):
    def one(a, carry):
        for k in range(0, 8, 2):
            out = jnp.dot(weights, pair_of(src, a, k), preferred_element_type=F32).astype(BF)
            for side in (0, 1):
                for comp in (0, 1):
                    block = out[NORB * comp : NORB * (comp + 1), NORB * side : NORB * (side + 1)]
                    dst[a, comp, k + side] = block.reshape(16, 8, NORB)
        return carry

    lax.fori_loop(0, 2, one, 0)


def self_energy_block(rows, cols, sigma, a, block):
    row_re, row_im = rows[a, 0, :, block].astype(F32), rows[a, 1, :, block].astype(F32)
    col_re, col_im = cols[a, 0, :, block].astype(F32), cols[a, 1, :, block].astype(F32)
    square_re = row_re * row_re - row_im * row_im
    square_im = 2.0 * row_re * row_im
    sigma[a, 0, :, block] = (square_re * col_re - square_im * col_im).astype(BF)
    sigma[a, 1, :, block] = (square_re * col_im + square_im * col_re).astype(BF)


def self_energy_all(rows, cols, sigma):
    def one(block, carry):
        for a in (0, 1):
            self_energy_block(rows, cols, sigma, a, block)
        return carry

    lax.fori_loop(0, 16, one, 0)


def collision_of(sigma, cols):
    totals = []
    for a in (0, 1):
        total = None
        for k in range(0, 8, 2):
            term = lax.dot_general(
                pair_of(sigma, a, k),
                pair_of(cols, a, k),
                (((1,), (1,)), ((), ())),
                preferred_element_type=F32,
            )
            total = term if total is None else total + term
        totals.append(total)
    rr, ri, ir, ii = parts_of(totals[0] - totals[1], 0)
    return step_length * (rr - ii), step_length * (ri + ir)


def all_copied(ref, sem):
    pltpu.make_async_copy(ref, ref, sem).wait()


def kernel(
    less_row, less_col, great_row, great_col, rho_ref, ham_ref,
    less_row_out, less_col_out, great_row_out, great_col_out, rho_out, residual_out,
    row_in, rows0, rows1, rows2, cols0, cols1, cols2, cols3, sigma, row_back,
    scat_src, scat, mid, gath, tiny_col, tiny_hist,
    in_send, in_recv, local_sem, row_sem, out_send, out_recv, back_sem,
    scat_send, scat_recv, mid_send, mid_recv, gath_send, gath_recv, tiny_send, tiny_recv,
):
    me_col, me_hist = lax.axis_index("col"), lax.axis_index("hist")
    me_z, me_core = me_col // 2, lax.rem(me_col, 2)

    def col_peer(dz, dc):
        return lax.rem(me_z + dz, 8) * 2 + lax.rem(me_core + dc, 2)

    def hist_peers(act):
        def one(offset, carry):
            act(lax.rem(me_hist + offset, 32))
            return carry

        lax.fori_loop(1, 32, one, 0)

    def push(src, dst, send, recv, axis, peer):
        pltpu.make_async_remote_copy(
            src_ref=src, dst_ref=dst, send_sem=send, recv_sem=recv,
            device_id={axis: peer}, device_id_type=MESH,
        ).start()

    barrier = pltpu.get_barrier_semaphore()
    for dz, dc in COL_PEERS:
        pl.semaphore_signal(
            barrier, inc=1, device_id={"col": col_peer(dz, dc)}, device_id_type=MESH
        )
    hist_peers(
        lambda p: pl.semaphore_signal(barrier, inc=1, device_id={"hist": p}, device_id_type=MESH)
    )
    row_refs, col_refs = (great_row, less_row), (less_col, great_col)
    for a in (0, 1):
        pltpu.make_async_copy(row_refs[a], row_in.at[a], row_sem).start()
        pltpu.make_async_copy(
            col_refs[a].at[:, pl.ds(me_col * 8, 8)], cols0.at[a, :, :, me_col], local_sem
        ).start()
    pl.semaphore_wait(barrier, 46)

    for dz, dc in COL_PEERS:
        peer = col_peer(dz, dc)
        for a in (0, 1):
            push(
                col_refs[a].at[:, pl.ds(peer * 8, 8)], cols0.at[a, :, :, me_col],
                in_send, in_recv.at[me_col], "col", peer,
            )

    eye_at = lax.broadcasted_iota(jnp.int32, (NORB, NORB), 0) == lax.broadcasted_iota(
        jnp.int32, (NORB, NORB), 1
    )
    eye = jnp.where(eye_at, 1.0, 0.0).astype(F32)
    hamiltonian = ham_ref[...]
    halved = (0.25 * step_length) * (hamiltonian + hamiltonian.T)
    off = jnp.where(eye_at, 0.0, halved)
    mean = step_length * 0.5 * mean_field

    def diagonals(matrix):
        kept = jnp.where(eye_at, matrix, 0.0)
        return jnp.sum(kept, axis=0, keepdims=True), jnp.sum(kept, axis=1, keepdims=True)

    def unitary_of(density_re):
        row, col = diagonals(halved + mean * density_re)
        return crank_nicolson(eye, off, row, col), col

    unit1, diag1 = unitary_of(rho_ref[0])
    weight_rows1, weight_cols1 = stacked_low(unit1, 1.0), stacked_low(unit1, -1.0)
    residual = residual_of(eye, off, diag1, unit1)
    rotated1 = rotate(unit1, (rho_ref[0], rho_ref[1]))

    all_copied(row_in, row_sem)

    def turn_in(block, carry):
        for a in (0, 1):
            for comp in (0, 1):
                piece = row_in[a, comp, pl.ds(block * 8, 8)].astype(F32)
                rows0[a, comp, :, block] = jnp.swapaxes(piece, 0, 1).astype(BF)
        return carry

    lax.fori_loop(0, 16, turn_in, 0)
    advance(weight_rows1, rows0, rows1)

    all_copied(cols0.at[:, :, :, 0], local_sem)
    for a in (0, 1):
        self_energy_block(rows0, cols0, sigma, a, me_col)
    for dz, dc in COL_PEERS[::-1]:
        peer = col_peer(dz, dc)
        all_copied(cols0.at[:, :, :, 0], in_recv.at[peer])
        for a in (0, 1):
            self_energy_block(rows0, cols0, sigma, a, peer)

    def scatter_sum(r, matrix):
        for comp in (0, 1):
            scat_src[r, pl.ds(16 * comp, 16)] = matrix[comp].reshape(16, 8, NORB)
        hist_peers(
            lambda p: push(
                scat_src.at[r, p], scat.at[r, me_hist],
                scat_send.at[r], scat_recv.at[r], "hist", p,
            )
        )
        scat[r, me_hist] = scat_src[r, me_hist]

    def middle_sum(r):
        all_copied(scat.at[r, pl.ds(0, 31)], scat_recv.at[r])
        mid[r, me_col] = jnp.sum(scat[r], axis=0)
        for dz, dc in COL_PEERS:
            push(
                mid.at[r, me_col], mid.at[r, me_col],
                mid_send.at[r], mid_recv.at[r], "col", col_peer(dz, dc),
            )

    def gather_sum(r):
        all_copied(mid.at[r, pl.ds(0, 15)], mid_recv.at[r])
        gath[r, me_hist] = jnp.sum(mid[r], axis=0)
        hist_peers(
            lambda p: push(
                gath.at[r, me_hist], gath.at[r, me_hist],
                gath_send.at[r], gath_recv.at[r], "hist", p,
            )
        )

    def summed(r):
        all_copied(gath.at[r, pl.ds(0, 31)], gath_recv.at[r])
        return tuple(gath[r, pl.ds(16 * comp, 16)].reshape(NORB, NORB) for comp in (0, 1))

    scatter_sum(0, collision_of(sigma, cols0))
    advance(weight_cols1, cols0, cols1)
    self_energy_all(rows1, cols1, sigma)
    second = collision_of(sigma, cols1)
    middle_sum(0)
    tiny_col[me_col] = jnp.sum(jnp.where(eye_at, second[0], 0.0), axis=0, keepdims=True)
    for dz, dc in COL_PEERS:
        push(
            tiny_col.at[me_col], tiny_col.at[me_col],
            tiny_send.at[0], tiny_recv.at[0], "col", col_peer(dz, dc),
        )
    gather_sum(0)
    all_copied(tiny_col.at[pl.ds(0, 15)], tiny_recv.at[0])
    tiny_hist[me_hist] = jnp.sum(tiny_col[...], axis=0)
    hist_peers(
        lambda p: push(
            tiny_hist.at[me_hist], tiny_hist.at[me_hist],
            tiny_send.at[1], tiny_recv.at[1], "hist", p,
        )
    )
    first = summed(0)

    density1 = (rotated1[0] + first[0], rotated1[1] + first[1])
    unit2, diag2 = unitary_of(density1[0])
    weight_rows2, weight_cols2 = stacked_low(unit2, 1.0), stacked_low(unit2, -1.0)
    rotated2 = rotate(unit2, density1)
    all_copied(tiny_hist.at[pl.ds(0, 31)], tiny_recv.at[1])
    second_diag = jnp.sum(tiny_hist[...], axis=0)
    unit3, diag3 = unitary_of(rotated2[0] + jnp.where(eye_at, second_diag, 0.0))
    weight_rows3, weight_cols3 = stacked_low(unit3, 1.0), stacked_low(unit3, -1.0)

    advance(weight_cols2, cols1, cols2)
    advance(weight_cols3, cols2, cols3)
    col_outs, row_outs = (less_col_out, great_col_out), (great_row_out, less_row_out)
    for dz, dc in COL_PEERS:
        peer = col_peer(dz, dc)
        for a in (0, 1):
            push(
                cols3.at[a, :, :, peer], col_outs[a].at[:, pl.ds(me_col * 8, 8)],
                out_send, out_recv.at[a], "col", peer,
            )
    for a in (0, 1):
        pltpu.make_async_copy(
            cols3.at[a, :, :, me_col], col_outs[a].at[:, pl.ds(me_col * 8, 8)], local_sem
        ).start()

    advance(weight_rows2, rows1, rows2)
    self_energy_all(rows2, cols2, sigma)
    third = collision_of(sigma, cols2)
    turned = rotate(unit3, second)
    scatter_sum(1, (turned[0] + third[0], turned[1] + third[1]))
    advance(weight_rows3, rows2, rows0)
    middle_sum(1)

    def turn_out(block, carry):
        for a in (0, 1):
            for comp in (0, 1):
                piece = rows0[a, comp, :, block].astype(F32)
                row_back[a, comp, pl.ds(block * 8, 8)] = jnp.swapaxes(piece, 0, 1).astype(BF)
        return carry

    lax.fori_loop(0, 16, turn_out, 0)
    for a in (0, 1):
        pltpu.make_async_copy(row_back.at[a], row_outs[a], back_sem).start()
    gather_sum(1)
    residual = jnp.maximum(residual, residual_of(eye, off, diag2, unit2))
    residual = jnp.maximum(residual, residual_of(eye, off, diag3, unit3))
    residual_out[...] = jnp.broadcast_to(residual, (8, NORB))
    rotated3 = rotate(unit3, rotated2)
    last = summed(1)
    for comp in (0, 1):
        rho_out[comp] = rotated3[comp] + last[comp]

    for r in (0, 1):
        all_copied(scat_src.at[r, pl.ds(0, 31)], scat_send.at[r])
        all_copied(mid.at[r, pl.ds(0, 15)], mid_send.at[r])
        all_copied(gath.at[r, pl.ds(0, 31)], gath_send.at[r])
    all_copied(tiny_col.at[pl.ds(0, 15)], tiny_send.at[0])
    all_copied(tiny_hist.at[pl.ds(0, 31)], tiny_send.at[1])
    all_copied(cols0.at[:, :, :, pl.ds(0, 15)], in_send)
    all_copied(cols3.at[:, :, :, 0], local_sem)
    all_copied(row_back, back_sem)
    all_copied(cols3.at[:, :, :, pl.ds(0, 15)], out_send)
    for a in (0, 1):
        all_copied(cols3.at[a, :, :, pl.ds(0, 15)], out_recv.at[a])


def per_device(less_row, less_col, great_row, great_col, density, hamiltonian):
    history = jax.ShapeDtypeStruct(less_row.shape, BF)
    planes = pltpu.VMEM((2, 2, 8, 16, 8, NORB), BF)
    dma = pltpu.SemaphoreType.DMA
    hbm = pl.BlockSpec(memory_space=pltpu.HBM)
    vmem = pl.BlockSpec(memory_space=pltpu.VMEM)
    *fast, residual = pl.pallas_call(
        kernel,
        out_shape=(history,) * 4
        + (
            jax.ShapeDtypeStruct(density.shape, F32),
            jax.ShapeDtypeStruct((8, NORB), F32),
        ),
        in_specs=[hbm] * 4 + [vmem] * 2,
        out_specs=(hbm,) * 4 + (vmem,) * 2,
        scratch_shapes=[
            pltpu.VMEM((2, *less_row.shape), BF),
            *[planes] * 8,
            pltpu.VMEM((2, *less_row.shape), BF),
            pltpu.VMEM((2, 32, 8, NORB), F32),
            pltpu.VMEM((2, 32, 8, NORB), F32),
            pltpu.VMEM((2, 16, 8, NORB), F32),
            pltpu.VMEM((2, 32, 8, NORB), F32),
            pltpu.VMEM((16, 1, NORB), F32),
            pltpu.VMEM((32, 1, NORB), F32),
            dma, dma((16,)), dma, dma, dma, dma((2,)), dma,
            *[dma((2,))] * 8,
        ],
        compiler_params=pltpu.CompilerParams(
            collective_id=0, has_side_effects=True, vmem_limit_bytes=48 * 2**20
        ),
        cost_estimate=pl.CostEstimate(flops=4 * 10**9, bytes_accessed=8 * 2**20, transcendentals=0),
    )(less_row, less_col, great_row, great_col, density, hamiltonian)
    return lax.cond(
        residual[0, 0] < RESIDUAL_MAX,
        lambda done, given: done,
        lambda done, given: direct_steps(*given),
        tuple(fast),
        (less_row, less_col, great_row, great_col, density, hamiltonian),
    )


def solution(mesh):
    in_specs = (
        P(None, None, "col", "hist"),
        P(None, None, "col", "hist"),
        P(None, None, "col", "hist"),
        P(None, None, "col", "hist"),
        P(),
        P(),
    )
    out_specs = (
        P(None, None, "col", "hist"),
        P(None, None, "col", "hist"),
        P(None, None, "col", "hist"),
        P(None, None, "col", "hist"),
        P(),
    )
    return jax.shard_map(
        per_device, mesh=mesh, in_specs=in_specs, out_specs=out_specs, check_vma=False
    )
```

```python
import jax
import jax.numpy as jnp
from jax import lax
from jax.experimental import pallas as pl
from jax.experimental.pallas import tpu as pltpu
from jax.sharding import PartitionSpec as P

STEPS = 3


step_length = 0.1
mean_field = 2.0
coupling = 1.0


def in_one_piece(arrays, axis, split_dim, concat_dim, along):
    ends, at = ([], 0)
    for a in arrays[:-1]:
        at += a.shape[along]
        ends.append(at)
    both = jnp.concatenate(arrays, axis=along)
    return tuple(
        jnp.split(
            lax.all_to_all(both, axis, split_axis=split_dim, concat_axis=concat_dim, tiled=True),
            ends,
            axis=along,
        )
    )


def split_up(array, dim, size):
    lengths = array.shape
    parts = array.reshape(*lengths[:dim], size, lengths[dim] // size, *lengths[dim + 1 :])
    return jnp.moveaxis(parts, dim, 0)


def summed_on_arrival(array, axis, dim):
    size = lax.axis_size(axis)
    parts = lax.all_to_all(split_up(array, dim, size), axis, 0, 0, tiled=True)
    return jnp.sum(parts.astype(jnp.float32), axis=0)


def from_everyone(array, axis):
    size = lax.axis_size(axis)
    return lax.all_to_all(
        jnp.broadcast_to(array[None], (size, *array.shape)), axis, 0, 0, tiled=True
    )


def over_copies(array, axis):
    return from_everyone(array, axis).sum(axis=0)


def joined_along(parts, dim):
    parts = jnp.moveaxis(parts, 0, dim)
    lengths = parts.shape
    return parts.reshape(*lengths[:dim], lengths[dim] * lengths[dim + 1], *lengths[dim + 2 :])


def gather_directly(array, axis, dim):
    return joined_along(from_everyone(array, axis), dim)


def unitary(hamiltonian, density):
    sym_ham = 0.5 * (hamiltonian + hamiltonian.T) + mean_field * jnp.diag(jnp.diagonal(density[0]))
    halved = 0.5 * step_length * sym_ham
    squared = jnp.dot(halved, halved, precision=lax.Precision.HIGHEST)
    identity = jnp.eye(sym_ham.shape[0], dtype=jnp.float32)
    factor = jnp.linalg.cholesky(identity + squared)
    unit_real = jax.scipy.linalg.cho_solve((factor, True), identity - squared)
    unit_imag = jax.scipy.linalg.cho_solve((factor, True), -2.0 * halved)
    return (unit_real, unit_imag)


def self_energy(row_hist, col_turned):
    green_real = row_hist[0].astype(jnp.float32)
    green_imag = row_hist[1].astype(jnp.float32)
    other_real = col_turned[0].astype(jnp.float32)
    other_imag = col_turned[1].astype(jnp.float32)
    square_real = green_real * green_real - green_imag * green_imag
    square_imag = 2.0 * green_real * green_imag
    out_real = coupling * coupling * (square_real * other_real - square_imag * other_imag)
    out_imag = coupling * coupling * (square_real * other_imag + square_imag * other_real)
    return jnp.stack([out_real, out_imag]).astype(jnp.bfloat16)


def contract_pair(first, second):
    return jnp.einsum("ikt,kjt->ij", first, second, preferred_element_type=jnp.float32)


def contract(sigma, rows_block):
    real_part = contract_pair(sigma[0], rows_block[0]) - contract_pair(sigma[1], rows_block[1])
    imag_part = contract_pair(sigma[0], rows_block[1]) + contract_pair(sigma[1], rows_block[0])
    return jnp.stack([real_part, imag_part])


def rotate_density(unit_real, unit_imag, rho):
    high = lax.Precision.HIGHEST
    left_real = jnp.dot(unit_real, rho[0], precision=high) - jnp.dot(
        unit_imag, rho[1], precision=high
    )
    left_imag = jnp.dot(unit_real, rho[1], precision=high) + jnp.dot(
        unit_imag, rho[0], precision=high
    )
    out_real = jnp.dot(left_real, unit_real.T, precision=high) + jnp.dot(
        left_imag, unit_imag.T, precision=high
    )
    out_imag = jnp.dot(left_imag, unit_real.T, precision=high) - jnp.dot(
        left_real, unit_imag.T, precision=high
    )
    return jnp.stack([out_real, out_imag])


def advance_rows(low_real, low_imag, history):
    count = history.shape[1]
    hist_real = history[0].reshape(count, -1)
    hist_imag = history[1].reshape(count, -1)
    out_real = jnp.dot(low_real, hist_real, preferred_element_type=jnp.float32) - jnp.dot(
        low_imag, hist_imag, preferred_element_type=jnp.float32
    )
    out_imag = jnp.dot(low_real, hist_imag, preferred_element_type=jnp.float32) + jnp.dot(
        low_imag, hist_real, preferred_element_type=jnp.float32
    )
    return jnp.stack([out_real, out_imag]).astype(jnp.bfloat16).reshape(history.shape)


def right_pair(first, matrix):
    return jnp.einsum("imt,jm->ijt", first, matrix, preferred_element_type=jnp.float32)


def advance_cols(low_real, low_imag, rows_block):
    out_real = right_pair(rows_block[0], low_real) + right_pair(rows_block[1], low_imag)
    out_imag = right_pair(rows_block[1], low_real) - right_pair(rows_block[0], low_imag)
    return jnp.stack([out_real, out_imag]).astype(jnp.bfloat16)


def direct_steps(less_row, less_col, great_row, great_col, density, hamiltonian):
    rho = density
    rows_less, rows_great = in_one_piece((less_col, great_col), "col", 1, 2, 0)
    for step_index in range(STEPS):
        unit_real, unit_imag = unitary(hamiltonian, rho)
        sigma_less = self_energy(less_row, jnp.swapaxes(rows_great, 1, 2))
        sigma_great = self_energy(great_row, jnp.swapaxes(rows_less, 1, 2))
        partial_sum = step_length * (
            contract(sigma_great, rows_less) - contract(sigma_less, rows_great)
        )
        rotated = rotate_density(unit_real, unit_imag, rho)
        column_piece = summed_on_arrival(partial_sum.astype(jnp.bfloat16), "col", 2)
        column_piece = over_copies(column_piece, "hist")
        width = column_piece.shape[2]
        start = lax.axis_index("col") * width
        own_block = lax.dynamic_slice_in_dim(rotated, start, width, 2) + column_piece
        rho = gather_directly(own_block, "col", 2)
        low_real = unit_real.astype(jnp.bfloat16)
        low_imag = unit_imag.astype(jnp.bfloat16)
        less_row = advance_rows(low_real, low_imag, less_row)
        great_row = advance_rows(low_real, low_imag, great_row)
        rows_less = advance_cols(low_real, low_imag, rows_less)
        rows_great = advance_cols(low_real, low_imag, rows_great)
    less_col, great_col = (
        lax.all_to_all(rows_less, "col", split_axis=2, concat_axis=1, tiled=True),
        lax.all_to_all(rows_great, "col", split_axis=2, concat_axis=1, tiled=True),
    )
    return (less_row, less_col, great_row, great_col, rho)


NORB = 128
BF = jnp.bfloat16
F32 = jnp.float32
MESH = pl.DeviceIdType.MESH
COL_PEERS = [(dz, dc) for dz in (4, 3, 5, 2, 6, 1, 7) for dc in (0, 1)] + [(0, 1)]
RESIDUAL_MAX = 3e-4
EARLY = 3


def split_terms(x):
    high = x.astype(BF)
    return high, (x - high.astype(F32)).astype(BF)


def fine_dot(a, b):
    ah, al = split_terms(a)
    bh, bl = split_terms(b)

    def one(p, q):
        return jnp.dot(p, q, preferred_element_type=F32)

    return one(ah, bh) + (one(ah, bl) + one(al, bh))


def parts_of(product, at):
    rr = product[at : at + NORB, :NORB]
    ri = product[at : at + NORB, NORB:]
    ir = product[at + NORB : at + 2 * NORB, :NORB]
    ii = product[at + NORB : at + 2 * NORB, NORB:]
    return rr, ri, ir, ii


def complex_dots(lefts, right):
    rows = jnp.concatenate([x for left in lefts for x in left], axis=0)
    product = fine_dot(rows, jnp.concatenate(right, axis=1))
    outs = []
    for n in range(len(lefts)):
        rr, ri, ir, ii = parts_of(product, 2 * NORB * n)
        outs.append((rr - ii, ri + ir))
    return outs


def rotate(unit, rho):
    left = complex_dots([unit], rho)[0]
    product = fine_dot(jnp.concatenate(left, axis=0), jnp.concatenate(unit, axis=1))
    rr, ri, ir, ii = parts_of(product, 0)
    return rr + ii, ir - ri


def crank_nicolson(eye, off, diag_row, diag_col):
    inv_re_col = 1.0 / (1.0 + diag_col * diag_col)
    inv_im_col = -diag_col * inv_re_col
    inv_re_row = 1.0 / (1.0 + diag_row * diag_row)
    inv_im_row = -diag_row * inv_re_row
    power = (inv_im_col * off, -inv_re_col * off)
    total = (eye + power[0], power[1])
    power = complex_dots([power], power)[0]
    for last in (False, False, True):
        if last:
            gain = complex_dots([total], power)[0]
        else:
            following, gain = complex_dots([power, total], power)
            power = following
        total = (total[0] + gain[0], total[1] + gain[1])
    inverse = (
        total[0] * inv_re_row - total[1] * inv_im_row,
        total[0] * inv_im_row + total[1] * inv_re_row,
    )
    return (2.0 * inverse[0] - eye, 2.0 * inverse[1])


def residual_of(eye, off, diag_col, unit):
    inverse = (0.5 * (unit[0] + eye), 0.5 * unit[1])
    rows = off + eye * diag_col
    product = fine_dot(rows, jnp.concatenate(inverse, axis=1))
    rest_re = inverse[0] - product[:, NORB:] - eye
    rest_im = inverse[1] + product[:, :NORB]
    sums = jnp.sum(jnp.abs(rest_re) + jnp.abs(rest_im), axis=1, keepdims=True)
    return jnp.max(sums, axis=0, keepdims=True)


def stacked_low(unit, sign):
    low_re, low_im = unit[0].astype(BF), (sign * unit[1]).astype(BF)
    top = jnp.concatenate([low_re, -low_im], axis=1)
    bottom = jnp.concatenate([low_im, low_re], axis=1)
    return jnp.concatenate([top, bottom], axis=0)


def pair_of(ref, a, k):
    sides = []
    for kk in (k, k + 1):
        planes = [ref[a, comp, kk].reshape(NORB, NORB) for comp in (0, 1)]
        sides.append(jnp.concatenate(planes, axis=0))
    return jnp.concatenate(sides, axis=1)


def advance(weights, src, dst, arrays=(0, 1)):
    def one(a, carry):
        for k in range(0, 8, 2):
            out = jnp.dot(weights, pair_of(src, a, k), preferred_element_type=F32).astype(BF)
            for side in (0, 1):
                for comp in (0, 1):
                    block = out[NORB * comp : NORB * (comp + 1), NORB * side : NORB * (side + 1)]
                    dst[a, comp, k + side] = block.reshape(16, 8, NORB)
        return carry

    if len(arrays) == 2:
        lax.fori_loop(0, 2, one, 0)
    else:
        one(arrays[0], 0)


def self_energy_block(rows, cols, sigma, a, block):
    row_re, row_im = rows[a, 0, :, block].astype(F32), rows[a, 1, :, block].astype(F32)
    col_re, col_im = cols[a, 0, :, block].astype(F32), cols[a, 1, :, block].astype(F32)
    square_re = row_re * row_re - row_im * row_im
    square_im = 2.0 * row_re * row_im
    sigma[a, 0, :, block] = (square_re * col_re - square_im * col_im).astype(BF)
    sigma[a, 1, :, block] = (square_re * col_im + square_im * col_re).astype(BF)


def self_energy_all(rows, cols, sigma):
    def one(block, carry):
        for a in (0, 1):
            self_energy_block(rows, cols, sigma, a, block)
        return carry

    lax.fori_loop(0, 16, one, 0)


def collision_of(sigma, cols):
    totals = []
    for a in (0, 1):
        total = None
        for k in range(0, 8, 2):
            term = lax.dot_general(
                pair_of(sigma, a, k),
                pair_of(cols, a, k),
                (((1,), (1,)), ((), ())),
                preferred_element_type=F32,
            )
            total = term if total is None else total + term
        totals.append(total)
    rr, ri, ir, ii = parts_of(totals[0] - totals[1], 0)
    return step_length * (rr - ii), step_length * (ri + ir)


def all_copied(ref, sem):
    pltpu.make_async_copy(ref, ref, sem).wait()


def kernel(
    less_row, less_col, great_row, great_col, rho_ref, ham_ref,
    less_row_out, less_col_out, great_row_out, great_col_out, rho_out, residual_out,
    row_in, col_in, rows0, rows1, rows2, cols0, cols1, cols2, cols3, sigma, row_back,
    scat_src0, scat0, mid0, gath0, scat_src1, scat1, mid1, gath1, tiny_col, tiny_hist,
    in_send, in_recv, local_sem, row_sem, col_sem, out_send, out_recv, back_sem,
    sum_send, sum_recv,
):
    me_col, me_hist = lax.axis_index("col"), lax.axis_index("hist")
    me_z, me_core = me_col // 2, lax.rem(me_col, 2)

    def col_peer(dz, dc):
        return lax.rem(me_z + dz, 8) * 2 + lax.rem(me_core + dc, 2)

    def hist_peers(act):
        def one(offset, carry):
            act(lax.rem(me_hist + offset, 32))
            return carry

        lax.fori_loop(1, 32, one, 0)

    def push(src, dst, send, recv, axis, peer):
        pltpu.make_async_remote_copy(
            src_ref=src, dst_ref=dst, send_sem=send, recv_sem=recv,
            device_id={axis: peer}, device_id_type=MESH,
        ).start()

    drains = []
    barrier = pltpu.get_barrier_semaphore()
    for dz, dc in COL_PEERS:
        pl.semaphore_signal(
            barrier, inc=1, device_id={"col": col_peer(dz, dc)}, device_id_type=MESH
        )
    hist_peers(
        lambda p: pl.semaphore_signal(barrier, inc=1, device_id={"hist": p}, device_id_type=MESH)
    )
    row_refs, col_refs = (great_row, less_row), (less_col, great_col)
    for a in (0, 1):
        pltpu.make_async_copy(col_refs[a], col_in.at[a], col_sem).start()
    for a in (0, 1):
        pltpu.make_async_copy(row_refs[a], row_in.at[a], row_sem).start()
    all_copied(col_in, col_sem)
    for a in (0, 1):
        pltpu.make_async_copy(
            col_in.at[a, :, pl.ds(me_col * 8, 8)], cols0.at[a, :, :, me_col], local_sem
        ).start()
    pl.semaphore_wait(barrier, 46)

    for dz, dc in COL_PEERS:
        peer = col_peer(dz, dc)
        for a in (0, 1):
            push(
                col_in.at[a, :, pl.ds(peer * 8, 8)], cols0.at[a, :, :, me_col],
                in_send, in_recv.at[me_col], "col", peer,
            )
    drains.append(lambda: all_copied(cols0.at[:, :, :, pl.ds(0, 15)], in_send))

    eye_at = lax.broadcasted_iota(jnp.int32, (NORB, NORB), 0) == lax.broadcasted_iota(
        jnp.int32, (NORB, NORB), 1
    )
    eye = jnp.where(eye_at, 1.0, 0.0).astype(F32)
    hamiltonian = ham_ref[...]
    halved = (0.25 * step_length) * (hamiltonian + hamiltonian.T)
    off = jnp.where(eye_at, 0.0, halved)
    mean = step_length * 0.5 * mean_field

    def diagonals(matrix):
        kept = jnp.where(eye_at, matrix, 0.0)
        return jnp.sum(kept, axis=0, keepdims=True), jnp.sum(kept, axis=1, keepdims=True)

    def unitary_of(density_re):
        row, col = diagonals(halved + mean * density_re)
        return crank_nicolson(eye, off, row, col), col

    unit1, diag1 = unitary_of(rho_ref[0])
    weight_rows1, weight_cols1 = stacked_low(unit1, 1.0), stacked_low(unit1, -1.0)
    residual = residual_of(eye, off, diag1, unit1)
    rotated1 = rotate(unit1, (rho_ref[0], rho_ref[1]))

    all_copied(row_in, row_sem)

    def turn_in(block, carry):
        for a in (0, 1):
            for comp in (0, 1):
                piece = row_in[a, comp, pl.ds(block * 8, 8)].astype(F32)
                rows0[a, comp, :, block] = jnp.swapaxes(piece, 0, 1).astype(BF)
        return carry

    lax.fori_loop(0, 16, turn_in, 0)
    advance(weight_rows1, rows0, rows1)

    all_copied(cols0.at[:, :, :, 0], local_sem)
    for a in (0, 1):
        self_energy_block(rows0, cols0, sigma, a, me_col)
    for dz, dc in COL_PEERS[::-1]:
        peer = col_peer(dz, dc)
        all_copied(cols0.at[:, :, :, 0], in_recv.at[peer])
        for a in (0, 1):
            self_energy_block(rows0, cols0, sigma, a, peer)

    def scatter(source, target, send, recv):
        hist_peers(lambda p: push(source.at[p], target.at[me_hist], send, recv, "hist", p))
        target[me_hist] = source[me_hist]
        drains.append(lambda: all_copied(source.at[pl.ds(0, 31)], send))

    def give_all(buffer, value, send, recv, axis):
        me, count = (me_col, 15) if axis == "col" else (me_hist, 31)
        buffer[me] = value
        if axis == "col":
            for dz, dc in COL_PEERS:
                push(buffer.at[me], buffer.at[me], send, recv, axis, col_peer(dz, dc))
        else:
            hist_peers(lambda p: push(buffer.at[me], buffer.at[me], send, recv, axis, p))
        drains.append(lambda: all_copied(buffer.at[pl.ds(0, count)], send))

    def arrived(buffer, recv):
        all_copied(buffer.at[pl.ds(0, buffer.shape[0] - 1)], recv)

    def whole(buffer, rows):
        return tuple(
            buffer[pl.ds(16 * comp, 16), rows : rows + 8].reshape(NORB, NORB) for comp in (0, 1)
        )

    first = collision_of(sigma, cols0)
    give_all(tiny_col, diagonals(first[0])[0], sum_send.at[1], sum_recv.at[1], "col")
    for comp in (0, 1):
        scat_src0[pl.ds(16 * comp, 16)] = first[comp].reshape(16, 8, NORB).astype(BF)
    scatter(scat_src0, scat0, sum_send.at[0], sum_recv.at[0])
    advance(weight_cols1, cols0, cols1)
    self_energy_all(rows1, cols1, sigma)
    second = collision_of(sigma, cols1)
    for comp in (0, 1):
        scat_src1[pl.ds(16 * comp, 16), 0:8] = second[comp].reshape(16, 8, NORB).astype(BF)
    second_diag = jnp.broadcast_to(diagonals(second[0])[0], (8, NORB))
    arrived(scat0, sum_recv.at[0])
    piece = jnp.sum(scat0[...].astype(F32), axis=0)
    give_all(
        mid0, jnp.concatenate([piece, second_diag], axis=0), sum_send.at[2], sum_recv.at[2], "col"
    )
    arrived(tiny_col, sum_recv.at[1])
    give_all(
        tiny_hist, jnp.sum(tiny_col[...], axis=0), sum_send.at[3], sum_recv.at[3], "hist"
    )
    arrived(mid0, sum_recv.at[2])
    give_all(gath0, jnp.sum(mid0[...], axis=0), sum_send.at[4], sum_recv.at[4], "hist")
    arrived(tiny_hist, sum_recv.at[3])
    first_diag = jnp.sum(tiny_hist[...], axis=0)
    unit2, diag2 = unitary_of(rotated1[0] + jnp.where(eye_at, first_diag, 0.0))
    weight_rows2, weight_cols2 = stacked_low(unit2, 1.0), stacked_low(unit2, -1.0)
    advance(weight_cols2, cols1, cols2)
    advance(weight_rows2, rows1, rows2)
    self_energy_all(rows2, cols2, sigma)
    third = collision_of(sigma, cols2)
    for comp in (0, 1):
        scat_src1[pl.ds(16 * comp, 16), 8:16] = third[comp].reshape(16, 8, NORB).astype(BF)
    scatter(scat_src1, scat1, sum_send.at[5], sum_recv.at[5])

    arrived(gath0, sum_recv.at[4])
    first = whole(gath0, 0)
    second_diag = jnp.sum(gath0[:, 8:16], axis=0)[0:1]
    rotated2 = rotate(unit2, (rotated1[0] + first[0], rotated1[1] + first[1]))
    unit3, diag3 = unitary_of(rotated2[0] + jnp.where(eye_at, second_diag, 0.0))
    weight_rows3, weight_cols3 = stacked_low(unit3, 1.0), stacked_low(unit3, -1.0)

    col_outs, row_outs = (less_col_out, great_col_out), (great_row_out, less_row_out)
    returns = [(a, dz, dc) for a in (0, 1) for dz, dc in COL_PEERS]

    def give_back(some):
        for a, dz, dc in some:
            push(
                cols3.at[a, :, :, col_peer(dz, dc)], col_outs[a].at[:, pl.ds(me_col * 8, 8)],
                out_send, out_recv.at[a], "col", col_peer(dz, dc),
            )

    advance(weight_cols3, cols2, cols3, (0,))
    give_back(returns[:EARLY])
    advance(weight_cols3, cols2, cols3, (1,))
    for a in (0, 1):
        pltpu.make_async_copy(
            cols3.at[a, :, :, me_col], col_outs[a].at[:, pl.ds(me_col * 8, 8)], local_sem
        ).start()
        drains.append(lambda a=a: all_copied(cols3.at[a, :, :, pl.ds(0, 15)], out_recv.at[a]))
    drains.append(lambda: all_copied(cols3.at[:, :, :, 0], local_sem))
    drains.append(lambda: all_copied(cols3.at[:, :, :, pl.ds(0, 15)], out_send))

    arrived(scat1, sum_recv.at[5])
    pieces = jnp.sum(scat1[...].astype(F32), axis=0)
    give_all(mid1, pieces.astype(BF), sum_send.at[6], sum_recv.at[6], "col")
    give_back(returns[EARLY:])
    advance(weight_rows3, rows2, rows0)

    def turn_out(block, carry):
        for a in (0, 1):
            for comp in (0, 1):
                piece = rows0[a, comp, :, block].astype(F32)
                row_back[a, comp, pl.ds(block * 8, 8)] = jnp.swapaxes(piece, 0, 1).astype(BF)
        return carry

    lax.fori_loop(0, 16, turn_out, 0)
    for a in (0, 1):
        pltpu.make_async_copy(row_back.at[a], row_outs[a], back_sem).start()
    drains.append(lambda: all_copied(row_back, back_sem))
    arrived(mid1, sum_recv.at[6])
    pieces = jnp.sum(mid1[...].astype(F32), axis=0)
    give_all(gath1, pieces, sum_send.at[7], sum_recv.at[7], "hist")
    residual = jnp.maximum(residual, residual_of(eye, off, diag2, unit2))
    residual = jnp.maximum(residual, residual_of(eye, off, diag3, unit3))
    residual_out[...] = residual
    arrived(gath1, sum_recv.at[7])
    second, third = whole(gath1, 0), whole(gath1, 8)
    rotated3 = rotate(unit3, (rotated2[0] + second[0], rotated2[1] + second[1]))
    for comp in (0, 1):
        rho_out[comp] = rotated3[comp] + third[comp]

    for drain in drains:
        drain()


def unload(*refs):
    sources, targets, stops = refs[:5], refs[5:10], refs[10:15]
    in_sem, out_sem = refs[15:]
    ins = [pltpu.make_async_copy(sources[n], stops[n], in_sem.at[n]) for n in range(5)]
    outs = [pltpu.make_async_copy(stops[n], targets[n], out_sem.at[n]) for n in range(5)]
    for copy in ins:
        copy.start()
    for n in range(5):
        ins[n].wait()
        outs[n].start()
    for copy in outs:
        copy.wait()


def per_device(less_row, less_col, great_row, great_col, density, hamiltonian):
    history = jax.ShapeDtypeStruct(less_row.shape, BF)
    planes = pltpu.VMEM((2, 2, 8, 16, 8, NORB), BF)
    dma = pltpu.SemaphoreType.DMA
    hbm = pl.BlockSpec(memory_space=pltpu.HBM)
    vmem = pl.BlockSpec(memory_space=pltpu.VMEM)
    *fast, residual = pl.pallas_call(
        kernel,
        out_shape=(history,) * 4
        + (
            jax.ShapeDtypeStruct(density.shape, F32),
            jax.ShapeDtypeStruct((1, 1), F32),
        ),
        in_specs=[hbm] * 4 + [vmem] * 2,
        out_specs=(hbm,) * 4 + (vmem,) * 2,
        scratch_shapes=[
            *[pltpu.VMEM((2, *less_row.shape), BF)] * 2,
            *[planes] * 8,
            pltpu.VMEM((2, *less_row.shape), BF),
            pltpu.VMEM((32, 8, NORB), BF),
            pltpu.VMEM((32, 8, NORB), BF),
            pltpu.VMEM((16, 16, NORB), F32),
            pltpu.VMEM((32, 16, NORB), F32),
            pltpu.VMEM((32, 16, NORB), BF),
            pltpu.VMEM((32, 16, NORB), BF),
            pltpu.VMEM((16, 16, NORB), BF),
            pltpu.VMEM((32, 16, NORB), F32),
            pltpu.VMEM((16, 1, NORB), F32),
            pltpu.VMEM((32, 1, NORB), F32),
            dma, dma((16,)), dma, dma, dma, dma, dma((2,)), dma,
            dma((8,)), dma((8,)),
        ],
        compiler_params=pltpu.CompilerParams(
            collective_id=0, has_side_effects=True, vmem_limit_bytes=24 * 2**20
        ),
        cost_estimate=pl.CostEstimate(flops=4 * 10**9, bytes_accessed=8 * 2**20, transcendentals=0),
    )(less_row, less_col, great_row, great_col, density, hamiltonian)
    place = pl.pallas_call(
        unload,
        out_shape=tuple(jax.ShapeDtypeStruct(x.shape, x.dtype) for x in fast),
        in_specs=[hbm] * 5,
        out_specs=(hbm,) * 5,
        scratch_shapes=[
            *[pltpu.VMEM(x.shape, x.dtype) for x in fast],
            dma((5,)),
            dma((5,)),
        ],
        compiler_params=pltpu.CompilerParams(vmem_limit_bytes=60 * 2**20),
    )
    return lax.cond(
        residual[0, 0] < RESIDUAL_MAX,
        lambda done, given: tuple(place(*done)),
        lambda done, given: direct_steps(*given),
        tuple(fast),
        (less_row, less_col, great_row, great_col, density, hamiltonian),
    )


def solution(mesh):
    in_specs = (
        P(None, None, "col", "hist"),
        P(None, None, "col", "hist"),
        P(None, None, "col", "hist"),
        P(None, None, "col", "hist"),
        P(),
        P(),
    )
    out_specs = (
        P(None, None, "col", "hist"),
        P(None, None, "col", "hist"),
        P(None, None, "col", "hist"),
        P(None, None, "col", "hist"),
        P(),
    )
    return jax.shard_map(
        per_device, mesh=mesh, in_specs=in_specs, out_specs=out_specs, check_vma=False
    )
```

```python
import jax
import jax.numpy as jnp
from jax import lax
from jax.experimental import pallas as pl
from jax.experimental.pallas import tpu as pltpu
from jax.sharding import PartitionSpec as P

STEPS = 3


step_length = 0.1
mean_field = 2.0
coupling = 1.0


def in_one_piece(arrays, axis, split_dim, concat_dim, along):
    ends, at = ([], 0)
    for a in arrays[:-1]:
        at += a.shape[along]
        ends.append(at)
    both = jnp.concatenate(arrays, axis=along)
    return tuple(
        jnp.split(
            lax.all_to_all(both, axis, split_axis=split_dim, concat_axis=concat_dim, tiled=True),
            ends,
            axis=along,
        )
    )


def split_up(array, dim, size):
    lengths = array.shape
    parts = array.reshape(*lengths[:dim], size, lengths[dim] // size, *lengths[dim + 1 :])
    return jnp.moveaxis(parts, dim, 0)


def summed_on_arrival(array, axis, dim):
    size = lax.axis_size(axis)
    parts = lax.all_to_all(split_up(array, dim, size), axis, 0, 0, tiled=True)
    return jnp.sum(parts.astype(jnp.float32), axis=0)


def from_everyone(array, axis):
    size = lax.axis_size(axis)
    return lax.all_to_all(
        jnp.broadcast_to(array[None], (size, *array.shape)), axis, 0, 0, tiled=True
    )


def over_copies(array, axis):
    return from_everyone(array, axis).sum(axis=0)


def joined_along(parts, dim):
    parts = jnp.moveaxis(parts, 0, dim)
    lengths = parts.shape
    return parts.reshape(*lengths[:dim], lengths[dim] * lengths[dim + 1], *lengths[dim + 2 :])


def gather_directly(array, axis, dim):
    return joined_along(from_everyone(array, axis), dim)


def unitary(hamiltonian, density):
    sym_ham = 0.5 * (hamiltonian + hamiltonian.T) + mean_field * jnp.diag(jnp.diagonal(density[0]))
    halved = 0.5 * step_length * sym_ham
    squared = jnp.dot(halved, halved, precision=lax.Precision.HIGHEST)
    identity = jnp.eye(sym_ham.shape[0], dtype=jnp.float32)
    factor = jnp.linalg.cholesky(identity + squared)
    unit_real = jax.scipy.linalg.cho_solve((factor, True), identity - squared)
    unit_imag = jax.scipy.linalg.cho_solve((factor, True), -2.0 * halved)
    return (unit_real, unit_imag)


def self_energy(row_hist, col_turned):
    green_real = row_hist[0].astype(jnp.float32)
    green_imag = row_hist[1].astype(jnp.float32)
    other_real = col_turned[0].astype(jnp.float32)
    other_imag = col_turned[1].astype(jnp.float32)
    square_real = green_real * green_real - green_imag * green_imag
    square_imag = 2.0 * green_real * green_imag
    out_real = coupling * coupling * (square_real * other_real - square_imag * other_imag)
    out_imag = coupling * coupling * (square_real * other_imag + square_imag * other_real)
    return jnp.stack([out_real, out_imag]).astype(jnp.bfloat16)


def contract_pair(first, second):
    return jnp.einsum("ikt,kjt->ij", first, second, preferred_element_type=jnp.float32)


def contract(sigma, rows_block):
    real_part = contract_pair(sigma[0], rows_block[0]) - contract_pair(sigma[1], rows_block[1])
    imag_part = contract_pair(sigma[0], rows_block[1]) + contract_pair(sigma[1], rows_block[0])
    return jnp.stack([real_part, imag_part])


def rotate_density(unit_real, unit_imag, rho):
    high = lax.Precision.HIGHEST
    left_real = jnp.dot(unit_real, rho[0], precision=high) - jnp.dot(
        unit_imag, rho[1], precision=high
    )
    left_imag = jnp.dot(unit_real, rho[1], precision=high) + jnp.dot(
        unit_imag, rho[0], precision=high
    )
    out_real = jnp.dot(left_real, unit_real.T, precision=high) + jnp.dot(
        left_imag, unit_imag.T, precision=high
    )
    out_imag = jnp.dot(left_imag, unit_real.T, precision=high) - jnp.dot(
        left_real, unit_imag.T, precision=high
    )
    return jnp.stack([out_real, out_imag])


def advance_rows(low_real, low_imag, history):
    count = history.shape[1]
    hist_real = history[0].reshape(count, -1)
    hist_imag = history[1].reshape(count, -1)
    out_real = jnp.dot(low_real, hist_real, preferred_element_type=jnp.float32) - jnp.dot(
        low_imag, hist_imag, preferred_element_type=jnp.float32
    )
    out_imag = jnp.dot(low_real, hist_imag, preferred_element_type=jnp.float32) + jnp.dot(
        low_imag, hist_real, preferred_element_type=jnp.float32
    )
    return jnp.stack([out_real, out_imag]).astype(jnp.bfloat16).reshape(history.shape)


def right_pair(first, matrix):
    return jnp.einsum("imt,jm->ijt", first, matrix, preferred_element_type=jnp.float32)


def advance_cols(low_real, low_imag, rows_block):
    out_real = right_pair(rows_block[0], low_real) + right_pair(rows_block[1], low_imag)
    out_imag = right_pair(rows_block[1], low_real) - right_pair(rows_block[0], low_imag)
    return jnp.stack([out_real, out_imag]).astype(jnp.bfloat16)


def direct_steps(less_row, less_col, great_row, great_col, density, hamiltonian):
    rho = density
    rows_less, rows_great = in_one_piece((less_col, great_col), "col", 1, 2, 0)
    for step_index in range(STEPS):
        unit_real, unit_imag = unitary(hamiltonian, rho)
        sigma_less = self_energy(less_row, jnp.swapaxes(rows_great, 1, 2))
        sigma_great = self_energy(great_row, jnp.swapaxes(rows_less, 1, 2))
        partial_sum = step_length * (
            contract(sigma_great, rows_less) - contract(sigma_less, rows_great)
        )
        rotated = rotate_density(unit_real, unit_imag, rho)
        column_piece = summed_on_arrival(partial_sum.astype(jnp.bfloat16), "col", 2)
        column_piece = over_copies(column_piece, "hist")
        width = column_piece.shape[2]
        start = lax.axis_index("col") * width
        own_block = lax.dynamic_slice_in_dim(rotated, start, width, 2) + column_piece
        rho = gather_directly(own_block, "col", 2)
        low_real = unit_real.astype(jnp.bfloat16)
        low_imag = unit_imag.astype(jnp.bfloat16)
        less_row = advance_rows(low_real, low_imag, less_row)
        great_row = advance_rows(low_real, low_imag, great_row)
        rows_less = advance_cols(low_real, low_imag, rows_less)
        rows_great = advance_cols(low_real, low_imag, rows_great)
    less_col, great_col = (
        lax.all_to_all(rows_less, "col", split_axis=2, concat_axis=1, tiled=True),
        lax.all_to_all(rows_great, "col", split_axis=2, concat_axis=1, tiled=True),
    )
    return (less_row, less_col, great_row, great_col, rho)


NORB = 128
BF = jnp.bfloat16
F32 = jnp.float32
MESH = pl.DeviceIdType.MESH
COL_PEERS = [(dz, dc) for dz in (4, 3, 5, 2, 6, 1, 7) for dc in (0, 1)] + [(0, 1)]
RESIDUAL_MAX = 3e-4
EARLY = 3


def split_terms(x):
    high = x.astype(BF)
    return high, (x - high.astype(F32)).astype(BF)


def fine_dot(a, b):
    ah, al = split_terms(a)
    bh, bl = split_terms(b)

    def one(p, q):
        return jnp.dot(p, q, preferred_element_type=F32)

    return one(ah, bh) + (one(ah, bl) + one(al, bh))


def parts_of(product, at):
    rr = product[at : at + NORB, :NORB]
    ri = product[at : at + NORB, NORB:]
    ir = product[at + NORB : at + 2 * NORB, :NORB]
    ii = product[at + NORB : at + 2 * NORB, NORB:]
    return rr, ri, ir, ii


def complex_dots(lefts, right):
    rows = jnp.concatenate([x for left in lefts for x in left], axis=0)
    product = fine_dot(rows, jnp.concatenate(right, axis=1))
    outs = []
    for n in range(len(lefts)):
        rr, ri, ir, ii = parts_of(product, 2 * NORB * n)
        outs.append((rr - ii, ri + ir))
    return outs


def rotate(unit, rho):
    left = complex_dots([unit], rho)[0]
    product = fine_dot(jnp.concatenate(left, axis=0), jnp.concatenate(unit, axis=1))
    rr, ri, ir, ii = parts_of(product, 0)
    return rr + ii, ir - ri


def crank_nicolson(eye, off, diag_row, diag_col):
    inv_re_col = 1.0 / (1.0 + diag_col * diag_col)
    inv_im_col = -diag_col * inv_re_col
    inv_re_row = 1.0 / (1.0 + diag_row * diag_row)
    inv_im_row = -diag_row * inv_re_row
    power = (inv_im_col * off, -inv_re_col * off)
    total = (eye + power[0], power[1])
    power = complex_dots([power], power)[0]
    for last in (False, True):
        if last:
            gain = complex_dots([total], power)[0]
        else:
            following, gain = complex_dots([power, total], power)
            power = following
        total = (total[0] + gain[0], total[1] + gain[1])
    inverse = (
        total[0] * inv_re_row - total[1] * inv_im_row,
        total[0] * inv_im_row + total[1] * inv_re_row,
    )
    return (2.0 * inverse[0] - eye, 2.0 * inverse[1])


def residual_of(eye, off, diag_col, unit):
    inverse = (0.5 * (unit[0] + eye), 0.5 * unit[1])
    rows = off + eye * diag_col
    product = fine_dot(rows, jnp.concatenate(inverse, axis=1))
    rest_re = inverse[0] - product[:, NORB:] - eye
    rest_im = inverse[1] + product[:, :NORB]
    sums = jnp.sum(jnp.abs(rest_re) + jnp.abs(rest_im), axis=1, keepdims=True)
    return jnp.max(sums, axis=0, keepdims=True)


def stacked_low(unit, sign):
    low_re, low_im = unit[0].astype(BF), (sign * unit[1]).astype(BF)
    top = jnp.concatenate([low_re, -low_im], axis=1)
    bottom = jnp.concatenate([low_im, low_re], axis=1)
    return jnp.concatenate([top, bottom], axis=0)


def pair_of(ref, a, k):
    sides = []
    for kk in (k, k + 1):
        planes = [ref[a, comp, kk].reshape(NORB, NORB) for comp in (0, 1)]
        sides.append(jnp.concatenate(planes, axis=0))
    return jnp.concatenate(sides, axis=1)


def advance(weights, src, dst, arrays=(0, 1)):
    def one(a, carry):
        for k in range(0, 8, 2):
            out = jnp.dot(weights, pair_of(src, a, k), preferred_element_type=F32).astype(BF)
            for side in (0, 1):
                for comp in (0, 1):
                    block = out[NORB * comp : NORB * (comp + 1), NORB * side : NORB * (side + 1)]
                    dst[a, comp, k + side] = block.reshape(16, 8, NORB)
        return carry

    if len(arrays) == 2:
        lax.fori_loop(0, 2, one, 0)
    else:
        one(arrays[0], 0)


def self_energy_block(rows, cols, sigma, a, block):
    row_re, row_im = rows[a, 0, :, block].astype(F32), rows[a, 1, :, block].astype(F32)
    col_re, col_im = cols[a, 0, :, block].astype(F32), cols[a, 1, :, block].astype(F32)
    square_re = row_re * row_re - row_im * row_im
    square_im = 2.0 * row_re * row_im
    sigma[a, 0, :, block] = (square_re * col_re - square_im * col_im).astype(BF)
    sigma[a, 1, :, block] = (square_re * col_im + square_im * col_re).astype(BF)


def self_energy_all(rows, cols, sigma):
    def one(block, carry):
        for a in (0, 1):
            self_energy_block(rows, cols, sigma, a, block)
        return carry

    lax.fori_loop(0, 16, one, 0)


def collision_of(sigma, cols):
    totals = []
    for a in (0, 1):
        total = None
        for k in range(0, 8, 2):
            term = lax.dot_general(
                pair_of(sigma, a, k),
                pair_of(cols, a, k),
                (((1,), (1,)), ((), ())),
                preferred_element_type=F32,
            )
            total = term if total is None else total + term
        totals.append(total)
    rr, ri, ir, ii = parts_of(totals[0] - totals[1], 0)
    return step_length * (rr - ii), step_length * (ri + ir)


def all_copied(ref, sem):
    pltpu.make_async_copy(ref, ref, sem).wait()


def kernel(
    less_row, less_col, great_row, great_col, rho_ref, ham_ref,
    less_row_out, less_col_out, great_row_out, great_col_out, rho_out, residual_out,
    row_in, col_in, rows0, rows1, rows2, cols0, cols1, cols2, cols3, sigma, row_back,
    scat_src0, scat0, mid0, gath0, scat_src1, scat1, mid1, gath1, tiny_col, tiny_hist,
    in_send, in_recv, local_sem, row_sem, col_sem, out_send, out_recv, back_sem,
    sum_send, sum_recv,
):
    me_col, me_hist = lax.axis_index("col"), lax.axis_index("hist")
    me_z, me_core = me_col // 2, lax.rem(me_col, 2)

    def col_peer(dz, dc):
        return lax.rem(me_z + dz, 8) * 2 + lax.rem(me_core + dc, 2)

    def hist_peers(act):
        def one(offset, carry):
            act(lax.rem(me_hist + offset, 32))
            return carry

        lax.fori_loop(1, 32, one, 0)

    def push(src, dst, send, recv, axis, peer):
        pltpu.make_async_remote_copy(
            src_ref=src, dst_ref=dst, send_sem=send, recv_sem=recv,
            device_id={axis: peer}, device_id_type=MESH,
        ).start()

    drains = []
    barrier = pltpu.get_barrier_semaphore()
    for dz, dc in COL_PEERS:
        pl.semaphore_signal(
            barrier, inc=1, device_id={"col": col_peer(dz, dc)}, device_id_type=MESH
        )
    hist_peers(
        lambda p: pl.semaphore_signal(barrier, inc=1, device_id={"hist": p}, device_id_type=MESH)
    )
    row_refs, col_refs = (great_row, less_row), (less_col, great_col)
    for a in (0, 1):
        pltpu.make_async_copy(col_refs[a], col_in.at[a], col_sem).start()
    for a in (0, 1):
        pltpu.make_async_copy(row_refs[a], row_in.at[a], row_sem).start()
    all_copied(col_in, col_sem)
    for a in (0, 1):
        pltpu.make_async_copy(
            col_in.at[a, :, pl.ds(me_col * 8, 8)], cols0.at[a, :, :, me_col], local_sem
        ).start()
    pl.semaphore_wait(barrier, 46)

    for dz, dc in COL_PEERS:
        peer = col_peer(dz, dc)
        for a in (0, 1):
            push(
                col_in.at[a, :, pl.ds(peer * 8, 8)], cols0.at[a, :, :, me_col],
                in_send, in_recv.at[me_col], "col", peer,
            )
    drains.append(lambda: all_copied(cols0.at[:, :, :, pl.ds(0, 15)], in_send))

    eye_at = lax.broadcasted_iota(jnp.int32, (NORB, NORB), 0) == lax.broadcasted_iota(
        jnp.int32, (NORB, NORB), 1
    )
    eye = jnp.where(eye_at, 1.0, 0.0).astype(F32)
    hamiltonian = ham_ref[...]
    halved = (0.25 * step_length) * (hamiltonian + hamiltonian.T)
    off = jnp.where(eye_at, 0.0, halved)
    mean = step_length * 0.5 * mean_field

    def diagonals(matrix):
        kept = jnp.where(eye_at, matrix, 0.0)
        return jnp.sum(kept, axis=0, keepdims=True), jnp.sum(kept, axis=1, keepdims=True)

    def unitary_of(density_re):
        row, col = diagonals(halved + mean * density_re)
        return crank_nicolson(eye, off, row, col), col

    unit1, diag1 = unitary_of(rho_ref[0])
    weight_rows1, weight_cols1 = stacked_low(unit1, 1.0), stacked_low(unit1, -1.0)
    residual = residual_of(eye, off, diag1, unit1)
    rotated1 = rotate(unit1, (rho_ref[0], rho_ref[1]))

    all_copied(row_in, row_sem)

    def turn_in(block, carry):
        for a in (0, 1):
            for comp in (0, 1):
                piece = row_in[a, comp, pl.ds(block * 8, 8)].astype(F32)
                rows0[a, comp, :, block] = jnp.swapaxes(piece, 0, 1).astype(BF)
        return carry

    lax.fori_loop(0, 16, turn_in, 0)
    advance(weight_rows1, rows0, rows1)

    all_copied(cols0.at[:, :, :, 0], local_sem)
    for a in (0, 1):
        self_energy_block(rows0, cols0, sigma, a, me_col)
    for dz, dc in COL_PEERS[::-1]:
        peer = col_peer(dz, dc)
        all_copied(cols0.at[:, :, :, 0], in_recv.at[peer])
        for a in (0, 1):
            self_energy_block(rows0, cols0, sigma, a, peer)

    def scatter(source, target, send, recv):
        hist_peers(lambda p: push(source.at[p], target.at[me_hist], send, recv, "hist", p))
        target[me_hist] = source[me_hist]
        drains.append(lambda: all_copied(source.at[pl.ds(0, 31)], send))

    def give_all(buffer, value, send, recv, axis):
        me, count = (me_col, 15) if axis == "col" else (me_hist, 31)
        buffer[me] = value
        if axis == "col":
            for dz, dc in COL_PEERS:
                push(buffer.at[me], buffer.at[me], send, recv, axis, col_peer(dz, dc))
        else:
            hist_peers(lambda p: push(buffer.at[me], buffer.at[me], send, recv, axis, p))
        drains.append(lambda: all_copied(buffer.at[pl.ds(0, count)], send))

    def arrived(buffer, recv):
        all_copied(buffer.at[pl.ds(0, buffer.shape[0] - 1)], recv)

    def whole(buffer, rows):
        return tuple(
            buffer[pl.ds(16 * comp, 16)].astype(F32)[:, rows : rows + 8].reshape(NORB, NORB)
            for comp in (0, 1)
        )

    first = collision_of(sigma, cols0)
    give_all(tiny_col, diagonals(first[0])[0], sum_send.at[1], sum_recv.at[1], "col")
    for comp in (0, 1):
        scat_src0[pl.ds(16 * comp, 16)] = first[comp].reshape(16, 8, NORB).astype(BF)
    scatter(scat_src0, scat0, sum_send.at[0], sum_recv.at[0])
    advance(weight_cols1, cols0, cols1)
    self_energy_all(rows1, cols1, sigma)
    second = collision_of(sigma, cols1)
    for comp in (0, 1):
        scat_src1[pl.ds(16 * comp, 16), 0:8] = second[comp].reshape(16, 8, NORB).astype(BF)
    second_diag = diagonals(second[0])[0]
    upper = lax.broadcasted_iota(jnp.int32, (8, NORB), 0) < 4

    def with_diagonal(piece, diag):
        high, low = split_terms(jnp.broadcast_to(diag, (8, NORB)))
        tail = jnp.where(upper, high.astype(F32), low.astype(F32))
        return jnp.concatenate([piece, tail], axis=0).astype(BF)

    def diagonal_in(total):
        return total[8:9] + total[12:13]

    arrived(scat0, sum_recv.at[0])
    piece = jnp.sum(scat0[...].astype(F32), axis=0)
    give_all(mid0, with_diagonal(piece, second_diag), sum_send.at[2], sum_recv.at[2], "col")
    arrived(tiny_col, sum_recv.at[1])
    give_all(
        tiny_hist, jnp.sum(tiny_col[...], axis=0), sum_send.at[3], sum_recv.at[3], "hist"
    )
    arrived(mid0, sum_recv.at[2])
    total = jnp.sum(mid0[...].astype(F32), axis=0)
    give_all(
        gath0, with_diagonal(total[0:8], diagonal_in(total)), sum_send.at[4], sum_recv.at[4], "hist"
    )
    arrived(tiny_hist, sum_recv.at[3])
    first_diag = jnp.sum(tiny_hist[...], axis=0)
    unit2, diag2 = unitary_of(rotated1[0] + jnp.where(eye_at, first_diag, 0.0))
    weight_rows2, weight_cols2 = stacked_low(unit2, 1.0), stacked_low(unit2, -1.0)
    advance(weight_cols2, cols1, cols2)
    advance(weight_rows2, rows1, rows2)
    self_energy_all(rows2, cols2, sigma)
    third = collision_of(sigma, cols2)
    for comp in (0, 1):
        scat_src1[pl.ds(16 * comp, 16), 8:16] = third[comp].reshape(16, 8, NORB).astype(BF)
    scatter(scat_src1, scat1, sum_send.at[5], sum_recv.at[5])

    arrived(gath0, sum_recv.at[4])
    first = whole(gath0, 0)
    second_diag = diagonal_in(jnp.sum(gath0[...].astype(F32), axis=0))
    rotated2 = rotate(unit2, (rotated1[0] + first[0], rotated1[1] + first[1]))
    unit3, diag3 = unitary_of(rotated2[0] + jnp.where(eye_at, second_diag, 0.0))
    weight_rows3, weight_cols3 = stacked_low(unit3, 1.0), stacked_low(unit3, -1.0)

    col_outs, row_outs = (less_col_out, great_col_out), (great_row_out, less_row_out)
    returns = [(a, dz, dc) for a in (0, 1) for dz, dc in COL_PEERS]

    def give_back(some):
        for a, dz, dc in some:
            push(
                cols3.at[a, :, :, col_peer(dz, dc)], col_outs[a].at[:, pl.ds(me_col * 8, 8)],
                out_send, out_recv.at[a], "col", col_peer(dz, dc),
            )

    advance(weight_cols3, cols2, cols3, (0,))
    give_back(returns[:EARLY])
    advance(weight_cols3, cols2, cols3, (1,))
    for a in (0, 1):
        pltpu.make_async_copy(
            cols3.at[a, :, :, me_col], col_outs[a].at[:, pl.ds(me_col * 8, 8)], local_sem
        ).start()
        drains.append(lambda a=a: all_copied(cols3.at[a, :, :, pl.ds(0, 15)], out_recv.at[a]))
    drains.append(lambda: all_copied(cols3.at[:, :, :, 0], local_sem))
    drains.append(lambda: all_copied(cols3.at[:, :, :, pl.ds(0, 15)], out_send))

    arrived(scat1, sum_recv.at[5])
    pieces = jnp.sum(scat1[...].astype(F32), axis=0)
    give_all(mid1, pieces.astype(BF), sum_send.at[6], sum_recv.at[6], "col")
    give_back(returns[EARLY:])
    advance(weight_rows3, rows2, rows0)

    def turn_out(block, carry):
        for a in (0, 1):
            for comp in (0, 1):
                piece = rows0[a, comp, :, block].astype(F32)
                row_back[a, comp, pl.ds(block * 8, 8)] = jnp.swapaxes(piece, 0, 1).astype(BF)
        return carry

    lax.fori_loop(0, 16, turn_out, 0)
    for a in (0, 1):
        pltpu.make_async_copy(row_back.at[a], row_outs[a], back_sem).start()
    drains.append(lambda: all_copied(row_back, back_sem))
    arrived(mid1, sum_recv.at[6])
    pieces = jnp.sum(mid1[...].astype(F32), axis=0)
    give_all(gath1, pieces, sum_send.at[7], sum_recv.at[7], "hist")
    residual = jnp.maximum(residual, residual_of(eye, off, diag2, unit2))
    residual = jnp.maximum(residual, residual_of(eye, off, diag3, unit3))
    residual_out[...] = residual
    arrived(gath1, sum_recv.at[7])
    second, third = whole(gath1, 0), whole(gath1, 8)
    rotated3 = rotate(unit3, (rotated2[0] + second[0], rotated2[1] + second[1]))
    for comp in (0, 1):
        rho_out[comp] = rotated3[comp] + third[comp]

    for drain in drains:
        drain()


def unload(*refs):
    sources, targets, stops = refs[:5], refs[5:10], refs[10:15]
    in_sem, out_sem = refs[15:]
    ins = [pltpu.make_async_copy(sources[n], stops[n], in_sem.at[n]) for n in range(5)]
    outs = [pltpu.make_async_copy(stops[n], targets[n], out_sem.at[n]) for n in range(5)]
    for copy in ins:
        copy.start()
    for n in range(5):
        ins[n].wait()
        outs[n].start()
    for copy in outs:
        copy.wait()


def per_device(less_row, less_col, great_row, great_col, density, hamiltonian):
    history = jax.ShapeDtypeStruct(less_row.shape, BF)
    planes = pltpu.VMEM((2, 2, 8, 16, 8, NORB), BF)
    dma = pltpu.SemaphoreType.DMA
    hbm = pl.BlockSpec(memory_space=pltpu.HBM)
    vmem = pl.BlockSpec(memory_space=pltpu.VMEM)
    *fast, residual = pl.pallas_call(
        kernel,
        out_shape=(history,) * 4
        + (
            jax.ShapeDtypeStruct(density.shape, F32),
            jax.ShapeDtypeStruct((1, 1), F32),
        ),
        in_specs=[hbm] * 4 + [vmem] * 2,
        out_specs=(hbm,) * 4 + (vmem,) * 2,
        scratch_shapes=[
            *[pltpu.VMEM((2, *less_row.shape), BF)] * 2,
            *[planes] * 8,
            pltpu.VMEM((2, *less_row.shape), BF),
            pltpu.VMEM((32, 8, NORB), BF),
            pltpu.VMEM((32, 8, NORB), BF),
            pltpu.VMEM((16, 16, NORB), BF),
            pltpu.VMEM((32, 16, NORB), BF),
            pltpu.VMEM((32, 16, NORB), BF),
            pltpu.VMEM((32, 16, NORB), BF),
            pltpu.VMEM((16, 16, NORB), BF),
            pltpu.VMEM((32, 16, NORB), F32),
            pltpu.VMEM((16, 1, NORB), F32),
            pltpu.VMEM((32, 1, NORB), F32),
            dma, dma((16,)), dma, dma, dma, dma, dma((2,)), dma,
            dma((8,)), dma((8,)),
        ],
        compiler_params=pltpu.CompilerParams(
            collective_id=0, has_side_effects=True, vmem_limit_bytes=24 * 2**20
        ),
        cost_estimate=pl.CostEstimate(flops=4 * 10**9, bytes_accessed=8 * 2**20, transcendentals=0),
    )(less_row, less_col, great_row, great_col, density, hamiltonian)
    place = pl.pallas_call(
        unload,
        out_shape=tuple(jax.ShapeDtypeStruct(x.shape, x.dtype) for x in fast),
        in_specs=[hbm] * 5,
        out_specs=(hbm,) * 5,
        scratch_shapes=[
            *[pltpu.VMEM(x.shape, x.dtype) for x in fast],
            dma((5,)),
            dma((5,)),
        ],
        compiler_params=pltpu.CompilerParams(vmem_limit_bytes=60 * 2**20),
    )
    return lax.cond(
        residual[0, 0] < RESIDUAL_MAX,
        lambda done, given: tuple(place(*done)),
        lambda done, given: direct_steps(*given),
        tuple(fast),
        (less_row, less_col, great_row, great_col, density, hamiltonian),
    )


def solution(mesh):
    in_specs = (
        P(None, None, "col", "hist"),
        P(None, None, "col", "hist"),
        P(None, None, "col", "hist"),
        P(None, None, "col", "hist"),
        P(),
        P(),
    )
    out_specs = (
        P(None, None, "col", "hist"),
        P(None, None, "col", "hist"),
        P(None, None, "col", "hist"),
        P(None, None, "col", "hist"),
        P(),
    )
    return jax.shard_map(
        per_device, mesh=mesh, in_specs=in_specs, out_specs=out_specs, check_vma=False
    )
```

```python
import jax
import jax.numpy as jnp
from jax import lax
from jax.experimental import pallas as pl
from jax.experimental.pallas import tpu as pltpu
from jax.sharding import PartitionSpec as P

STEPS = 3


step_length = 0.1
mean_field = 2.0
coupling = 1.0


def in_one_piece(arrays, axis, split_dim, concat_dim, along):
    ends, at = ([], 0)
    for a in arrays[:-1]:
        at += a.shape[along]
        ends.append(at)
    both = jnp.concatenate(arrays, axis=along)
    return tuple(
        jnp.split(
            lax.all_to_all(both, axis, split_axis=split_dim, concat_axis=concat_dim, tiled=True),
            ends,
            axis=along,
        )
    )


def split_up(array, dim, size):
    lengths = array.shape
    parts = array.reshape(*lengths[:dim], size, lengths[dim] // size, *lengths[dim + 1 :])
    return jnp.moveaxis(parts, dim, 0)


def summed_on_arrival(array, axis, dim):
    size = lax.axis_size(axis)
    parts = lax.all_to_all(split_up(array, dim, size), axis, 0, 0, tiled=True)
    return jnp.sum(parts.astype(jnp.float32), axis=0)


def from_everyone(array, axis):
    size = lax.axis_size(axis)
    return lax.all_to_all(
        jnp.broadcast_to(array[None], (size, *array.shape)), axis, 0, 0, tiled=True
    )


def over_copies(array, axis):
    return from_everyone(array, axis).sum(axis=0)


def joined_along(parts, dim):
    parts = jnp.moveaxis(parts, 0, dim)
    lengths = parts.shape
    return parts.reshape(*lengths[:dim], lengths[dim] * lengths[dim + 1], *lengths[dim + 2 :])


def gather_directly(array, axis, dim):
    return joined_along(from_everyone(array, axis), dim)


def unitary(hamiltonian, density):
    sym_ham = 0.5 * (hamiltonian + hamiltonian.T) + mean_field * jnp.diag(jnp.diagonal(density[0]))
    halved = 0.5 * step_length * sym_ham
    squared = jnp.dot(halved, halved, precision=lax.Precision.HIGHEST)
    identity = jnp.eye(sym_ham.shape[0], dtype=jnp.float32)
    factor = jnp.linalg.cholesky(identity + squared)
    unit_real = jax.scipy.linalg.cho_solve((factor, True), identity - squared)
    unit_imag = jax.scipy.linalg.cho_solve((factor, True), -2.0 * halved)
    return (unit_real, unit_imag)


def self_energy(row_hist, col_turned):
    green_real = row_hist[0].astype(jnp.float32)
    green_imag = row_hist[1].astype(jnp.float32)
    other_real = col_turned[0].astype(jnp.float32)
    other_imag = col_turned[1].astype(jnp.float32)
    square_real = green_real * green_real - green_imag * green_imag
    square_imag = 2.0 * green_real * green_imag
    out_real = coupling * coupling * (square_real * other_real - square_imag * other_imag)
    out_imag = coupling * coupling * (square_real * other_imag + square_imag * other_real)
    return jnp.stack([out_real, out_imag]).astype(jnp.bfloat16)


def contract_pair(first, second):
    return jnp.einsum("ikt,kjt->ij", first, second, preferred_element_type=jnp.float32)


def contract(sigma, rows_block):
    real_part = contract_pair(sigma[0], rows_block[0]) - contract_pair(sigma[1], rows_block[1])
    imag_part = contract_pair(sigma[0], rows_block[1]) + contract_pair(sigma[1], rows_block[0])
    return jnp.stack([real_part, imag_part])


def rotate_density(unit_real, unit_imag, rho):
    high = lax.Precision.HIGHEST
    left_real = jnp.dot(unit_real, rho[0], precision=high) - jnp.dot(
        unit_imag, rho[1], precision=high
    )
    left_imag = jnp.dot(unit_real, rho[1], precision=high) + jnp.dot(
        unit_imag, rho[0], precision=high
    )
    out_real = jnp.dot(left_real, unit_real.T, precision=high) + jnp.dot(
        left_imag, unit_imag.T, precision=high
    )
    out_imag = jnp.dot(left_imag, unit_real.T, precision=high) - jnp.dot(
        left_real, unit_imag.T, precision=high
    )
    return jnp.stack([out_real, out_imag])


def advance_rows(low_real, low_imag, history):
    count = history.shape[1]
    hist_real = history[0].reshape(count, -1)
    hist_imag = history[1].reshape(count, -1)
    out_real = jnp.dot(low_real, hist_real, preferred_element_type=jnp.float32) - jnp.dot(
        low_imag, hist_imag, preferred_element_type=jnp.float32
    )
    out_imag = jnp.dot(low_real, hist_imag, preferred_element_type=jnp.float32) + jnp.dot(
        low_imag, hist_real, preferred_element_type=jnp.float32
    )
    return jnp.stack([out_real, out_imag]).astype(jnp.bfloat16).reshape(history.shape)


def right_pair(first, matrix):
    return jnp.einsum("imt,jm->ijt", first, matrix, preferred_element_type=jnp.float32)


def advance_cols(low_real, low_imag, rows_block):
    out_real = right_pair(rows_block[0], low_real) + right_pair(rows_block[1], low_imag)
    out_imag = right_pair(rows_block[1], low_real) - right_pair(rows_block[0], low_imag)
    return jnp.stack([out_real, out_imag]).astype(jnp.bfloat16)


def direct_steps(less_row, less_col, great_row, great_col, density, hamiltonian):
    rho = density
    rows_less, rows_great = in_one_piece((less_col, great_col), "col", 1, 2, 0)
    for step_index in range(STEPS):
        unit_real, unit_imag = unitary(hamiltonian, rho)
        sigma_less = self_energy(less_row, jnp.swapaxes(rows_great, 1, 2))
        sigma_great = self_energy(great_row, jnp.swapaxes(rows_less, 1, 2))
        partial_sum = step_length * (
            contract(sigma_great, rows_less) - contract(sigma_less, rows_great)
        )
        rotated = rotate_density(unit_real, unit_imag, rho)
        column_piece = summed_on_arrival(partial_sum.astype(jnp.bfloat16), "col", 2)
        column_piece = over_copies(column_piece, "hist")
        width = column_piece.shape[2]
        start = lax.axis_index("col") * width
        own_block = lax.dynamic_slice_in_dim(rotated, start, width, 2) + column_piece
        rho = gather_directly(own_block, "col", 2)
        low_real = unit_real.astype(jnp.bfloat16)
        low_imag = unit_imag.astype(jnp.bfloat16)
        less_row = advance_rows(low_real, low_imag, less_row)
        great_row = advance_rows(low_real, low_imag, great_row)
        rows_less = advance_cols(low_real, low_imag, rows_less)
        rows_great = advance_cols(low_real, low_imag, rows_great)
    less_col, great_col = (
        lax.all_to_all(rows_less, "col", split_axis=2, concat_axis=1, tiled=True),
        lax.all_to_all(rows_great, "col", split_axis=2, concat_axis=1, tiled=True),
    )
    return (less_row, less_col, great_row, great_col, rho)


NORB = 128
BF = jnp.bfloat16
F32 = jnp.float32
MESH = pl.DeviceIdType.MESH
COL_PEERS = [(dz, dc) for dz in (4, 3, 5, 2, 6, 1, 7) for dc in (0, 1)] + [(0, 1)]
RESIDUAL_MAX = 3e-4
EARLY = 6


def split_terms(x):
    high = x.astype(BF)
    return high, (x - high.astype(F32)).astype(BF)


def fine_dot(a, b):
    ah, al = split_terms(a)
    bh, bl = split_terms(b)

    def one(p, q):
        return jnp.dot(p, q, preferred_element_type=F32)

    return one(ah, bh) + (one(ah, bl) + one(al, bh))


def parts_of(product, at):
    rr = product[at : at + NORB, :NORB]
    ri = product[at : at + NORB, NORB:]
    ir = product[at + NORB : at + 2 * NORB, :NORB]
    ii = product[at + NORB : at + 2 * NORB, NORB:]
    return rr, ri, ir, ii


def complex_dots(lefts, right):
    rows = jnp.concatenate([x for left in lefts for x in left], axis=0)
    product = fine_dot(rows, jnp.concatenate(right, axis=1))
    outs = []
    for n in range(len(lefts)):
        rr, ri, ir, ii = parts_of(product, 2 * NORB * n)
        outs.append((rr - ii, ri + ir))
    return outs


def rotate(unit, rho):
    return rotate_right(complex_dots([unit], rho)[0], unit)


def rotate_right(left, unit):
    product = fine_dot(jnp.concatenate(left, axis=0), jnp.concatenate(unit, axis=1))
    rr, ri, ir, ii = parts_of(product, 0)
    return rr + ii, ir - ri


def crank_nicolson(eye, off, diag_row, diag_col):
    inv_re_col = 1.0 / (1.0 + diag_col * diag_col)
    inv_im_col = -diag_col * inv_re_col
    inv_re_row = 1.0 / (1.0 + diag_row * diag_row)
    inv_im_row = -diag_row * inv_re_row
    power = (inv_im_col * off, -inv_re_col * off)
    total = (eye + power[0], power[1])
    power = complex_dots([power], power)[0]
    for last in (False, True):
        if last:
            gain = complex_dots([total], power)[0]
        else:
            following, gain = complex_dots([power, total], power)
            power = following
        total = (total[0] + gain[0], total[1] + gain[1])
    inverse = (
        total[0] * inv_re_row - total[1] * inv_im_row,
        total[0] * inv_im_row + total[1] * inv_re_row,
    )
    return (2.0 * inverse[0] - eye, 2.0 * inverse[1])


def residual_of(eye, off, diag_col, unit):
    inverse = (0.5 * (unit[0] + eye), 0.5 * unit[1])
    rows = off + eye * diag_col
    product = fine_dot(rows, jnp.concatenate(inverse, axis=1))
    rest_re = inverse[0] - product[:, NORB:] - eye
    rest_im = inverse[1] + product[:, :NORB]
    sums = jnp.sum(jnp.abs(rest_re) + jnp.abs(rest_im), axis=1, keepdims=True)
    return jnp.max(sums, axis=0, keepdims=True)


def stacked_low(unit, sign):
    low_re, low_im = unit[0].astype(BF), (sign * unit[1]).astype(BF)
    top = jnp.concatenate([low_re, -low_im], axis=1)
    bottom = jnp.concatenate([low_im, low_re], axis=1)
    return jnp.concatenate([top, bottom], axis=0)


def pair_of(ref, a, k):
    sides = []
    for kk in (k, k + 1):
        planes = [ref[a, comp, kk].reshape(NORB, NORB) for comp in (0, 1)]
        sides.append(jnp.concatenate(planes, axis=0))
    return jnp.concatenate(sides, axis=1)


def advance(weights, src, dst, arrays=(0, 1)):
    def one(a, carry):
        for k in range(0, 8, 2):
            out = jnp.dot(weights, pair_of(src, a, k), preferred_element_type=F32).astype(BF)
            for side in (0, 1):
                for comp in (0, 1):
                    block = out[NORB * comp : NORB * (comp + 1), NORB * side : NORB * (side + 1)]
                    dst[a, comp, k + side] = block.reshape(16, 8, NORB)
        return carry

    if len(arrays) == 2:
        lax.fori_loop(0, 2, one, 0)
    else:
        one(arrays[0], 0)


def self_energy_block(rows, cols, sigma, a, block):
    row_re, row_im = rows[a, 0, :, block].astype(F32), rows[a, 1, :, block].astype(F32)
    col_re, col_im = cols[a, 0, :, block].astype(F32), cols[a, 1, :, block].astype(F32)
    square_re = row_re * row_re - row_im * row_im
    square_im = 2.0 * row_re * row_im
    sigma[a, 0, :, block] = (square_re * col_re - square_im * col_im).astype(BF)
    sigma[a, 1, :, block] = (square_re * col_im + square_im * col_re).astype(BF)


def self_energy_all(rows, cols, sigma):
    def one(block, carry):
        for a in (0, 1):
            self_energy_block(rows, cols, sigma, a, block)
        return carry

    lax.fori_loop(0, 16, one, 0)


def collision_of(sigma, cols):
    totals = []
    for a in (0, 1):
        total = None
        for k in range(0, 8, 2):
            term = lax.dot_general(
                pair_of(sigma, a, k),
                pair_of(cols, a, k),
                (((1,), (1,)), ((), ())),
                preferred_element_type=F32,
            )
            total = term if total is None else total + term
        totals.append(total)
    rr, ri, ir, ii = parts_of(totals[0] - totals[1], 0)
    return step_length * (rr - ii), step_length * (ri + ir)


def all_copied(ref, sem):
    pltpu.make_async_copy(ref, ref, sem).wait()


def kernel(
    less_row, less_col, great_row, great_col, rho_ref, ham_ref,
    less_row_out, less_col_out, great_row_out, great_col_out, rho_out, residual_out,
    row_in, col_in, rows0, rows1, rows2, cols0, cols1, cols2, cols3, sigma, row_back,
    scat_src0, scat0, mid0, gath0, scat_src1, scat1, mid1, gath1, tiny_col, tiny_hist,
    in_send, in_recv, local_sem, row_sem, col_sem, out_send, out_recv, back_sem,
    sum_send, sum_recv,
):
    me_col, me_hist = lax.axis_index("col"), lax.axis_index("hist")
    me_z, me_core = me_col // 2, lax.rem(me_col, 2)

    def col_peer(dz, dc):
        return lax.rem(me_z + dz, 8) * 2 + lax.rem(me_core + dc, 2)

    def hist_peers(act):
        def one(offset, carry):
            act(lax.rem(me_hist + offset, 32))
            return carry

        lax.fori_loop(1, 32, one, 0)

    def push(src, dst, send, recv, axis, peer):
        pltpu.make_async_remote_copy(
            src_ref=src, dst_ref=dst, send_sem=send, recv_sem=recv,
            device_id={axis: peer}, device_id_type=MESH,
        ).start()

    drains = []
    barrier = pltpu.get_barrier_semaphore()
    for dz, dc in COL_PEERS:
        pl.semaphore_signal(
            barrier, inc=1, device_id={"col": col_peer(dz, dc)}, device_id_type=MESH
        )
    hist_peers(
        lambda p: pl.semaphore_signal(barrier, inc=1, device_id={"hist": p}, device_id_type=MESH)
    )
    row_refs, col_refs = (great_row, less_row), (less_col, great_col)
    for a in (0, 1):
        pltpu.make_async_copy(col_refs[a], col_in.at[a], col_sem).start()
    for a in (0, 1):
        pltpu.make_async_copy(row_refs[a], row_in.at[a], row_sem).start()
    all_copied(col_in, col_sem)
    for a in (0, 1):
        pltpu.make_async_copy(
            col_in.at[a, :, pl.ds(me_col * 8, 8)], cols0.at[a, :, :, me_col], local_sem
        ).start()
    pl.semaphore_wait(barrier, 46)

    for dz, dc in COL_PEERS:
        peer = col_peer(dz, dc)
        for a in (0, 1):
            push(
                col_in.at[a, :, pl.ds(peer * 8, 8)], cols0.at[a, :, :, me_col],
                in_send, in_recv.at[me_col], "col", peer,
            )
    drains.append(lambda: all_copied(cols0.at[:, :, :, pl.ds(0, 15)], in_send))

    eye_at = lax.broadcasted_iota(jnp.int32, (NORB, NORB), 0) == lax.broadcasted_iota(
        jnp.int32, (NORB, NORB), 1
    )
    eye = jnp.where(eye_at, 1.0, 0.0).astype(F32)
    hamiltonian = ham_ref[...]
    halved = (0.25 * step_length) * (hamiltonian + hamiltonian.T)
    off = jnp.where(eye_at, 0.0, halved)
    mean = step_length * 0.5 * mean_field

    def diagonals(matrix):
        kept = jnp.where(eye_at, matrix, 0.0)
        return jnp.sum(kept, axis=0, keepdims=True), jnp.sum(kept, axis=1, keepdims=True)

    def unitary_of(density_re):
        row, col = diagonals(halved + mean * density_re)
        return crank_nicolson(eye, off, row, col), col

    unit1, diag1 = unitary_of(rho_ref[0])
    weight_rows1, weight_cols1 = stacked_low(unit1, 1.0), stacked_low(unit1, -1.0)
    residual = residual_of(eye, off, diag1, unit1)
    rotated1 = rotate(unit1, (rho_ref[0], rho_ref[1]))

    all_copied(row_in, row_sem)

    def turn_in(block, carry):
        for a in (0, 1):
            for comp in (0, 1):
                piece = row_in[a, comp, pl.ds(block * 8, 8)].astype(F32)
                rows0[a, comp, :, block] = jnp.swapaxes(piece, 0, 1).astype(BF)
        return carry

    lax.fori_loop(0, 16, turn_in, 0)
    advance(weight_rows1, rows0, rows1)

    all_copied(cols0.at[:, :, :, 0], local_sem)
    for a in (0, 1):
        self_energy_block(rows0, cols0, sigma, a, me_col)
    for dz, dc in COL_PEERS[::-1]:
        peer = col_peer(dz, dc)
        all_copied(cols0.at[:, :, :, 0], in_recv.at[peer])
        for a in (0, 1):
            self_energy_block(rows0, cols0, sigma, a, peer)

    def scatter(source, target, send, recv):
        hist_peers(lambda p: push(source.at[p], target.at[me_hist], send, recv, "hist", p))
        target[me_hist] = source[me_hist]
        drains.append(lambda: all_copied(source.at[pl.ds(0, 31)], send))

    def give_all(buffer, value, send, recv, axis):
        me, count = (me_col, 15) if axis == "col" else (me_hist, 31)
        buffer[me] = value
        if axis == "col":
            for dz, dc in COL_PEERS:
                push(buffer.at[me], buffer.at[me], send, recv, axis, col_peer(dz, dc))
        else:
            hist_peers(lambda p: push(buffer.at[me], buffer.at[me], send, recv, axis, p))
        drains.append(lambda: all_copied(buffer.at[pl.ds(0, count)], send))

    def arrived(buffer, recv):
        all_copied(buffer.at[pl.ds(0, buffer.shape[0] - 1)], recv)

    def whole(buffer, rows):
        return tuple(
            buffer[pl.ds(16 * comp, 16)].astype(F32)[:, rows : rows + 8].reshape(NORB, NORB)
            for comp in (0, 1)
        )

    first = collision_of(sigma, cols0)
    give_all(tiny_col, diagonals(first[0])[0], sum_send.at[1], sum_recv.at[1], "col")
    for comp in (0, 1):
        scat_src0[pl.ds(16 * comp, 16)] = first[comp].reshape(16, 8, NORB).astype(BF)
    scatter(scat_src0, scat0, sum_send.at[0], sum_recv.at[0])
    advance(weight_cols1, cols0, cols1)
    self_energy_all(rows1, cols1, sigma)
    second = collision_of(sigma, cols1)
    for comp in (0, 1):
        scat_src1[pl.ds(16 * comp, 16), 0:8] = second[comp].reshape(16, 8, NORB).astype(BF)
    second_diag = diagonals(second[0])[0]
    upper = lax.broadcasted_iota(jnp.int32, (8, NORB), 0) < 4

    def with_diagonal(piece, diag):
        high, low = split_terms(jnp.broadcast_to(diag, (8, NORB)))
        tail = jnp.where(upper, high.astype(F32), low.astype(F32))
        return jnp.concatenate([piece, tail], axis=0).astype(BF)

    def diagonal_in(total):
        return total[8:9] + total[12:13]

    arrived(scat0, sum_recv.at[0])
    piece = jnp.sum(scat0[...].astype(F32), axis=0)
    give_all(mid0, with_diagonal(piece, second_diag), sum_send.at[2], sum_recv.at[2], "col")
    arrived(tiny_col, sum_recv.at[1])
    give_all(
        tiny_hist, jnp.sum(tiny_col[...], axis=0), sum_send.at[3], sum_recv.at[3], "hist"
    )
    arrived(mid0, sum_recv.at[2])
    total = jnp.sum(mid0[...].astype(F32), axis=0)
    give_all(
        gath0, with_diagonal(total[0:8], diagonal_in(total)), sum_send.at[4], sum_recv.at[4], "hist"
    )
    arrived(tiny_hist, sum_recv.at[3])
    first_diag = jnp.sum(tiny_hist[...], axis=0)
    unit2, diag2 = unitary_of(rotated1[0] + jnp.where(eye_at, first_diag, 0.0))
    weight_rows2, weight_cols2 = stacked_low(unit2, 1.0), stacked_low(unit2, -1.0)
    advance(weight_cols2, cols1, cols2)
    advance(weight_rows2, rows1, rows2)
    self_energy_all(rows2, cols2, sigma)
    third = collision_of(sigma, cols2)
    for comp in (0, 1):
        scat_src1[pl.ds(16 * comp, 16), 8:16] = third[comp].reshape(16, 8, NORB).astype(BF)

    arrived(gath0, sum_recv.at[4])
    first = whole(gath0, 0)
    second_diag = diagonal_in(jnp.sum(gath0[...].astype(F32), axis=0))
    left2 = complex_dots([unit2], (rotated1[0] + first[0], rotated1[1] + first[1]))[0]
    turned_diag = jnp.sum(left2[0] * unit2[0] + left2[1] * unit2[1], axis=1, keepdims=True)
    unit3, diag3 = unitary_of(jnp.where(eye_at, turned_diag + second_diag, 0.0))
    weight_rows3, weight_cols3 = stacked_low(unit3, 1.0), stacked_low(unit3, -1.0)

    col_outs, row_outs = (less_col_out, great_col_out), (great_row_out, less_row_out)
    returns = [(a, dz, dc) for a in (0, 1) for dz, dc in COL_PEERS]

    def give_back(some):
        for a, dz, dc in some:
            push(
                cols3.at[a, :, :, col_peer(dz, dc)], col_outs[a].at[:, pl.ds(me_col * 8, 8)],
                out_send, out_recv.at[a], "col", col_peer(dz, dc),
            )

    advance(weight_cols3, cols2, cols3, (0,))
    give_back(returns[:EARLY])
    scatter(scat_src1, scat1, sum_send.at[5], sum_recv.at[5])
    advance(weight_cols3, cols2, cols3, (1,))
    for a in (0, 1):
        pltpu.make_async_copy(
            cols3.at[a, :, :, me_col], col_outs[a].at[:, pl.ds(me_col * 8, 8)], local_sem
        ).start()
        drains.append(lambda a=a: all_copied(cols3.at[a, :, :, pl.ds(0, 15)], out_recv.at[a]))
    drains.append(lambda: all_copied(cols3.at[:, :, :, 0], local_sem))
    drains.append(lambda: all_copied(cols3.at[:, :, :, pl.ds(0, 15)], out_send))

    arrived(scat1, sum_recv.at[5])
    pieces = jnp.sum(scat1[...].astype(F32), axis=0)
    give_all(mid1, pieces.astype(BF), sum_send.at[6], sum_recv.at[6], "col")
    give_back(returns[EARLY:])
    advance(weight_rows3, rows2, rows0)

    def turn_out(block, carry):
        for a in (0, 1):
            for comp in (0, 1):
                piece = rows0[a, comp, :, block].astype(F32)
                row_back[a, comp, pl.ds(block * 8, 8)] = jnp.swapaxes(piece, 0, 1).astype(BF)
        return carry

    lax.fori_loop(0, 16, turn_out, 0)
    for a in (0, 1):
        pltpu.make_async_copy(row_back.at[a], row_outs[a], back_sem).start()
    drains.append(lambda: all_copied(row_back, back_sem))
    arrived(mid1, sum_recv.at[6])
    pieces = jnp.sum(mid1[...].astype(F32), axis=0)
    give_all(gath1, pieces, sum_send.at[7], sum_recv.at[7], "hist")
    rotated2 = rotate_right(left2, unit2)
    residual = jnp.maximum(residual, residual_of(eye, off, diag2, unit2))
    residual = jnp.maximum(residual, residual_of(eye, off, diag3, unit3))
    residual_out[...] = residual
    arrived(gath1, sum_recv.at[7])
    second, third = whole(gath1, 0), whole(gath1, 8)
    rotated3 = rotate(unit3, (rotated2[0] + second[0], rotated2[1] + second[1]))
    for comp in (0, 1):
        rho_out[comp] = rotated3[comp] + third[comp]

    for drain in drains:
        drain()


def unload(*refs):
    sources, targets, sem = refs[:5], refs[5:10], refs[10]
    copies = [pltpu.make_async_copy(sources[n], targets[n], sem.at[n]) for n in range(5)]
    for copy in copies:
        copy.start()
    for copy in copies:
        copy.wait()


def per_device(less_row, less_col, great_row, great_col, density, hamiltonian):
    planes = pltpu.VMEM((2, 2, 8, 16, 8, NORB), BF)
    dma = pltpu.SemaphoreType.DMA
    hbm = pl.BlockSpec(memory_space=pltpu.HBM)
    vmem = pl.BlockSpec(memory_space=pltpu.VMEM)
    *fast, residual = pl.pallas_call(
        kernel,
        out_shape=(pltpu.VMEM(less_row.shape, BF),) * 4
        + (
            pltpu.VMEM(density.shape, F32),
            jax.ShapeDtypeStruct((1, 1), F32),
        ),
        in_specs=[hbm] * 4 + [vmem] * 2,
        out_specs=(vmem,) * 6,
        scratch_shapes=[
            *[pltpu.VMEM((2, *less_row.shape), BF)] * 2,
            *[planes] * 8,
            pltpu.VMEM((2, *less_row.shape), BF),
            pltpu.VMEM((32, 8, NORB), BF),
            pltpu.VMEM((32, 8, NORB), BF),
            pltpu.VMEM((16, 16, NORB), BF),
            pltpu.VMEM((32, 16, NORB), BF),
            pltpu.VMEM((32, 16, NORB), BF),
            pltpu.VMEM((32, 16, NORB), BF),
            pltpu.VMEM((16, 16, NORB), BF),
            pltpu.VMEM((32, 16, NORB), F32),
            pltpu.VMEM((16, 1, NORB), F32),
            pltpu.VMEM((32, 1, NORB), F32),
            dma, dma((16,)), dma, dma, dma, dma, dma((2,)), dma,
            dma((8,)), dma((8,)),
        ],
        compiler_params=pltpu.CompilerParams(
            collective_id=0, has_side_effects=True, vmem_limit_bytes=24 * 2**20
        ),
        cost_estimate=pl.CostEstimate(flops=4 * 10**9, bytes_accessed=8 * 2**20, transcendentals=0),
    )(less_row, less_col, great_row, great_col, density, hamiltonian)
    place = pl.pallas_call(
        unload,
        out_shape=tuple(jax.ShapeDtypeStruct(x.shape, x.dtype) for x in fast),
        in_specs=[vmem] * 5,
        out_specs=(hbm,) * 5,
        scratch_shapes=[dma((5,))],
        compiler_params=pltpu.CompilerParams(vmem_limit_bytes=4 * 2**20),
    )
    return lax.cond(
        residual[0, 0] < RESIDUAL_MAX,
        lambda done, given: tuple(place(*done)),
        lambda done, given: direct_steps(*given),
        tuple(fast),
        (less_row, less_col, great_row, great_col, density, hamiltonian),
    )


def solution(mesh):
    in_specs = (
        P(None, None, "col", "hist"),
        P(None, None, "col", "hist"),
        P(None, None, "col", "hist"),
        P(None, None, "col", "hist"),
        P(),
        P(),
    )
    out_specs = (
        P(None, None, "col", "hist"),
        P(None, None, "col", "hist"),
        P(None, None, "col", "hist"),
        P(None, None, "col", "hist"),
        P(),
    )
    return jax.shard_map(
        per_device, mesh=mesh, in_specs=in_specs, out_specs=out_specs, check_vma=False
    )
```
